256 devices in a mesh: vid: 32 (over z, y), head: 8 (over x, core).
Axes of the slice: x: 4, y: 4, z: 8, core: 2. Of those that a mesh axis runs over, the one named last changes fastest.
Arguments:
- queries: bfloat16 [2048, 8192], P('vid', 'head'), may hold values from -6 to 6
- out_grad: bfloat16 [2048, 8192], P('vid', 'head'), may hold values from -1024 to 1024
- log_totals: bfloat16 [64, 2048], P('head', 'vid'), as said below
- out_dots: bfloat16 [64, 2048], P('head', 'vid'), may hold values from -4096 to 4096
- lengths: int32 [32], replicated, may hold values from 1 to 64, 1024 in all
- vis_keys: bfloat16 [16384, 1024], P('vid', 'head'), may hold values from -6 to 6
- vis_values: bfloat16 [16384, 1024], P('vid', 'head'), may hold values from -6 to 6
- key_weight: bfloat16 [8192, 1024], P('head'), may hold values from -0.0625 to 0.0625
- value_weight: bfloat16 [8192, 1024], P('head'), may hold values from -0.0625 to 0.0625
- frame_owner: int32 [1024, 1], replicated, may hold values from 0 to 31; in each aligned block of 32 rows (0 to 31, 32 to 63, ...) at most 2 rows name the same one
Outputs:
- query_grad: bfloat16 [2048, 8192], P('vid', 'head')
- owned_grad: bfloat16 [32768, 8192], P('vid', 'head')
The draws below stay inside these ranges and needn't reach their ends.
Inputs may be any that keep to these rules, and one draw needn't show every extreme that they name: `lengths`: the entries sum to exactly 1024; rows t * 64 + lengths[t] to t * 64 + 63 of a thread are padding. `frame_owner`: in each aligned block of 32 frames, no owner is named more than 2 times. `log_totals`: each entry lies between log(16384) + 0.25 and log(16384) + 1.35.
All inputs are finite; a program needn't handle non-finite values.
Results may differ from the reference program's by a relative error of at most 0.0057.
Values may be sent and summed in bfloat16 or wider, within the bound.
No kernel may reach another device: no remote copies, remote signals or barrier semaphores. Data moves between devices by JAX's collectives and lax.ppermute only.
A program may use at most 128 MiB of HBM per device.

```python
import math
import jax
import jax.numpy as jnp
import numpy as np
from jax import lax

D = 8192
QH = 64
KVH = 8
HD = 128
QLEN = 64
TPF = 16
THREADS = 32
QROWS = 2048
LIVE = 1024
VIS = 16384
FPD = 32
FRAMES = 1024
MOST = 2
N_VID = 32


def draw_log_totals(key, part):
    key = jax.random.fold_in(key, 7)
    offset = jax.random.uniform(key, (QH, QROWS), jnp.float32, 0.3, 1.3)
    return (offset + math.log(VIS)).astype(jnp.bfloat16)


def shard_levels(stream_key, shape, split, low, largest):
    factor_of, own = 1.0, jax.random.fold_in(stream_key, 6)
    for dim, parts in split:
        heights = jnp.exp(jax.random.uniform(jax.random.fold_in(own, dim), (parts,), jnp.float32, low / len(split), largest / len(split)))
        factor_of = factor_of * jnp.repeat(heights, shape[dim] // parts).reshape([-1 if axis == dim else 1 for axis in range(len(shape))])
    return factor_of


def profile(amount, total, most, slope):
    loads = [(1 << 20) // math.isqrt(grade ** slope) + 1 for grade in range(2, amount + 1)]
    rest, counts = total - most - (amount - 1), [1] * (amount - 1)
    while rest > 0:
        free = [i for i in range(amount - 1) if counts[i] < most]
        mass, left = sum([loads[i] for i in free]), rest
        for i in free:
            extra = min(most - counts[i], max(1, left * loads[i] // mass), rest)
            counts[i] = counts[i] + extra
            rest = rest - extra
    return np.array([most] + counts)


def uneven(stream_key, amount, total, reach, lean):
    if amount == 2:
        one = jax.random.randint(stream_key, (), max(1, total - reach), min(reach, total - 1) + 1)
        return jnp.stack([one, total - one])
    sizes = jnp.asarray(profile(amount, total, reach, lean), jnp.int32)
    twos = (amount - 1) // 2
    donor, sink = sizes[1:1 + 2 * twos:2], sizes[2:2 + 2 * twos:2]
    margin = jnp.minimum(donor - 1, reach - sink)
    shifted = jax.random.randint(jax.random.fold_in(stream_key, 1), (twos,), 0, 1 << 20) % (margin + 1)
    sizes = sizes.at[1:1 + 2 * twos:2].set(donor - shifted).at[2:2 + 2 * twos:2].set(sink + shifted)
    return sizes[jax.random.permutation(jax.random.fold_in(stream_key, 2), amount)]


def deal_out(own_key, own, number, rows, number_of, top, most, slope):
    sequence = jax.random.permutation(own_key, number_of)
    heavy_load, ordinary = load_shares(number_of, rows * top, most, slope, True), load_shares(number_of, rows * top, most, slope, False)
    places = jnp.arange(number_of)

    def named(tallies, rotation):
        used = int((tallies > 0).sum())
        fixed = max(1, used // 4)
        passed = fixed + (places - fixed + rotation * (used - fixed)) % max(1, number_of - fixed)
        return jnp.zeros((number_of,), jnp.int32).at[sequence[jnp.where(places < fixed, places, passed)]].set(jnp.asarray(tallies, jnp.int32))

    tallies = jnp.where(number % 4 == 0, named(heavy_load, number // 4), named(ordinary, number - number // 4 - 1))
    mixed = jax.random.permutation(jax.random.fold_in(own, 3), number_of)
    source_of, sink = mixed[0:number_of // 2 * 2:2], mixed[1:number_of // 2 * 2:2]
    room = jnp.minimum(tallies[source_of] - 1, most - tallies[sink]) // 2
    room = jnp.where((source_of == sequence[0]) | (sink == sequence[0]) | (tallies[sink] == 0), 0, jnp.maximum(room, 0))
    passed = jax.random.randint(jax.random.fold_in(own, 4), (number_of // 2,), 0, 1 << 20) % (room + 1)
    tallies = tallies.at[source_of].add(-passed).at[sink].add(passed)
    members = jnp.searchsorted(jnp.cumsum(tallies), jnp.arange(rows * top), side="right").astype(jnp.int32)
    grid = members.reshape(top, rows).T
    grid = grid[jax.random.permutation(jax.random.fold_in(own, 1), rows)]
    rotation = jax.random.randint(jax.random.fold_in(own, 2), (rows, 1), 0, top)
    return jnp.take_along_axis(grid, (jnp.arange(top)[None, :] + rotation) % top, axis=1)


def load_shares(number_of, total, bound, skew, full):
    weights = [(1 << 20) // math.isqrt(grade ** skew) + 1 for grade in range(1, number_of + 1)]
    largest = bound if full else min(bound, max(-(-total // number_of), total * weights[0] // sum(weights)))
    least = 1 if total - largest >= number_of - 1 else 0
    holding, spare = [largest] + [least] * (number_of - 1), total - largest - least * (number_of - 1)
    while spare > 0:
        free = [i for i in range(1, number_of) if holding[i] < largest] or [i for i in range(1, number_of) if holding[i] < bound]
        pool, budget = sum([weights[i] for i in free]), spare
        for i in free:
            addition = min(bound - holding[i], max(1, budget * weights[i] // pool), spare)
            holding[i] = holding[i] + addition
            spare = spare - addition
    return np.array(holding)


def gaussian(rng, dims, scale, most, split=(), held_as=jnp.bfloat16):
    drawn = scale * jax.random.normal(rng, dims, jnp.float32)
    if split:
        drawn = drawn * shard_levels(rng, dims, split, -0.22, 0.18)
    return jnp.clip(drawn, -most, most).astype(held_as)


def setup_inputs(seed: int = 0) -> dict:
    key_list = jax.random.split(jax.random.key(seed), 11)
    queries = gaussian(key_list[0], (QROWS, QH * HD), 1.0, 6.0, ((0, 32), (1, 8)))
    out_grad = gaussian(key_list[1], (QROWS, QH * HD), (32 * THREADS ** 0.5), 1024.0, ((0, 32), (1, 8)))
    log_totals = draw_log_totals(jax.random.fold_in(key_list[10], 71), 0)
    out_dots = gaussian(key_list[3], (QH, QROWS), (10 * THREADS ** 0.5 * HD ** 0.5), 4096.0, ((0, 8), (1, 32)))
    lengths = uneven(key_list[4], THREADS, LIVE, QLEN, 2).astype(jnp.int32)
    vis_keys = gaussian(key_list[5], (VIS, KVH * HD), 1.0, 6.0, ((0, 32), (1, 8)))
    vis_values = gaussian(key_list[6], (VIS, KVH * HD), 1.0, 6.0, ((0, 32), (1, 8)))
    key_weight = gaussian(key_list[7], (D, KVH * HD), D ** -0.5, 0.0625, ((0, 8),))
    value_weight = gaussian(key_list[8], (D, KVH * HD), D ** -0.5, 0.0625, ((0, 8),))
    frame_owner_keys = jax.random.split(jax.random.fold_in(key_list[9], 1), FRAMES // FPD)
    frame_owner_turns = jax.random.permutation(jax.random.fold_in(key_list[9], 3), FRAMES // FPD)
    frame_owner = jax.vmap(lambda own, number: deal_out(jax.random.fold_in(key_list[9], 2), own, number, FPD, N_VID, 1, MOST, 2))(frame_owner_keys, frame_owner_turns).reshape((FRAMES, 1))
    return dict(queries=queries, out_grad=out_grad, log_totals=log_totals, out_dots=out_dots, lengths=lengths, vis_keys=vis_keys, vis_values=vis_values, key_weight=key_weight, value_weight=value_weight, frame_owner=frame_owner)


def live_rows(lengths):
    position = jnp.arange(QROWS, dtype=jnp.int32)
    thread = (position // QLEN).astype(jnp.int32)
    return ((position - thread * QLEN) < jnp.take(lengths, thread)).astype(jnp.float32)


def owner_slots(vis_grad, frame_owner):
    owners = frame_owner[:, 0].reshape(N_VID, FPD)
    onehot = (owners[:, :, None] == jnp.arange(N_VID, dtype=jnp.int32)[None, None, :]).astype(jnp.int32)
    before = (jnp.cumsum(onehot, axis=1) - onehot).astype(jnp.int32)
    slot_rank = jnp.sum(onehot * before, axis=2).astype(jnp.int32)
    chosen = onehot[:, :, :, None] * (slot_rank[:, :, None, None] == jnp.arange(MOST, dtype=jnp.int32)[None, None, None, :]).astype(jnp.int32)
    frame_ids = jnp.arange(FRAMES, dtype=jnp.int32).reshape(N_VID, FPD)
    frame_number = jnp.sum(chosen * frame_ids[:, :, None, None], axis=1).astype(jnp.int32)
    present = jnp.sum(chosen, axis=1).astype(jnp.int32)
    frame_number = frame_number.transpose(1, 0, 2).reshape(N_VID * N_VID * MOST)
    present = present.transpose(1, 0, 2).reshape(N_VID * N_VID * MOST)
    frames = vis_grad.reshape(FRAMES, TPF, D)
    picked = jnp.take(frames, frame_number, axis=0)
    picked = jnp.where(present[:, None, None] > 0, picked, jnp.zeros_like(picked))
    return picked.reshape(N_VID * N_VID * MOST * TPF, D)


def reference(queries, out_grad, log_totals, out_dots, lengths, vis_keys, vis_values, key_weight, value_weight, frame_owner):
    groups = QH // KVH
    score_scale = HD ** -0.5
    key_block = math.gcd(VIS, 1024)
    valid_rows = live_rows(lengths)
    query_heads = queries.astype(jnp.float32).reshape(QROWS, KVH, groups, HD).transpose(1, 0, 2, 3)
    grad_heads = out_grad.astype(jnp.float32).reshape(QROWS, KVH, groups, HD).transpose(1, 0, 2, 3)
    total_heads = log_totals.astype(jnp.float32).reshape(KVH, groups, QROWS)
    dot_heads = out_dots.astype(jnp.float32).reshape(KVH, groups, QROWS)
    key_heads = vis_keys.astype(jnp.float32).reshape(VIS // key_block, key_block, KVH, HD).transpose(2, 0, 1, 3)
    value_heads = vis_values.astype(jnp.float32).reshape(VIS // key_block, key_block, KVH, HD).transpose(2, 0, 1, 3)

    def one_head(operands):
        query_h, grad_h, total_h, dot_h, key_h, value_h = operands

        def block_step(query_acc, block):
            key_blk, value_blk = block
            scores = jnp.einsum('qgd,kd->gqk', query_h, key_blk) * score_scale
            probs = jnp.exp(scores - total_h[:, :, None]) * valid_rows[None, :, None]
            grad_probs = jnp.einsum('qgd,kd->gqk', grad_h, value_blk)
            grad_scores = probs * (grad_probs - dot_h[:, :, None])
            probs_b = lax.optimization_barrier(probs.astype(jnp.bfloat16)).astype(jnp.float32)
            scores_b = lax.optimization_barrier(grad_scores.astype(jnp.bfloat16)).astype(jnp.float32)
            grad_value = jnp.einsum('gqk,qgd->kd', probs_b, grad_h)
            grad_key = jnp.einsum('gqk,qgd->kd', scores_b, query_h) * score_scale
            query_acc = query_acc + jnp.einsum('gqk,kd->qgd', scores_b, key_blk) * score_scale
            return query_acc, (grad_key, grad_value)

        start = jnp.zeros((QROWS, groups, HD), jnp.float32)
        query_acc, (grad_key, grad_value) = lax.scan(block_step, start, (key_h, value_h))
        return query_acc, grad_key.reshape(VIS, HD), grad_value.reshape(VIS, HD)

    query_acc, grad_keys, grad_values = lax.map(one_head, (query_heads, grad_heads, total_heads, dot_heads, key_heads, value_heads))
    query_grad = query_acc.transpose(1, 0, 2, 3).reshape(QROWS, QH * HD).astype(jnp.bfloat16)
    key_grad = grad_keys.transpose(1, 0, 2).reshape(VIS, KVH * HD).astype(jnp.bfloat16)
    value_grad = grad_values.transpose(1, 0, 2).reshape(VIS, KVH * HD).astype(jnp.bfloat16)
    vis_grad = jnp.dot(key_grad, key_weight.T, preferred_element_type=jnp.float32)
    vis_grad = vis_grad + jnp.dot(value_grad, value_weight.T, preferred_element_type=jnp.float32)
    vis_grad = vis_grad.astype(jnp.bfloat16)
    return query_grad, owner_slots(vis_grad, frame_owner)
```

```python
import math

import jax
import jax.numpy as jnp
from jax import lax
from jax.experimental import pallas as pl
from jax.experimental.pallas import tpu as pltpu
from jax.sharding import PartitionSpec as P

QH = 64
KVH = 8
HD = 128
TPF = 16
QLEN = 64
GROUP = QH // KVH
ROWS = GROUP * QLEN
NZ = 8
NY = 4
NX = 4
BLOCK = 512
MSG = 2 * QLEN + 16
FPD = 32
MOST = 2
N_VID = NZ * NY
SLOT_ROWS = N_VID * MOST * TPF
SCALE = HD ** (-0.5)
LOG2E = math.log2(math.e)
DEAD = 1e30
TILE = 256
VMEM = 48 * 1024 * 1024


def shift_z(a, k):
    pairs = [(z * NY + y, ((z + k) % NZ) * NY + y) for z in range(NZ) for y in range(NY)]
    return lax.ppermute(a, "vid", pairs)


def shift_y(a, k):
    pairs = [(z * NY + y, z * NY + (y + k) % NY) for z in range(NZ) for y in range(NY)]
    return lax.ppermute(a, "vid", pairs)


def shift_x(a, k):
    pairs = [(x * 2 + c, ((x + k) % NX) * 2 + c) for x in range(NX) for c in range(2)]
    return lax.ppermute(a, "head", pairs)


def swap_core(a):
    pairs = [(x * 2 + c, x * 2 + 1 - c) for x in range(NX) for c in range(2)]
    return lax.ppermute(a, "head", pairs)


def pack_kernel(q_ref, g_ref, stat_ref, msg_ref):
    msg_ref[0:QLEN, :] = q_ref[...]
    msg_ref[QLEN : 2 * QLEN, :] = g_ref[...]
    msg_ref[2 * QLEN :, :] = jnp.broadcast_to(stat_ref[...], (16, 2 * ROWS))


def heads_as_rows(block):
    return jnp.concatenate([block[:, h * HD : (h + 1) * HD] for h in range(GROUP)], axis=0)


def attend(chunks, kv, acc, last):
    flat, split = [], []
    for chunk in chunks:
        parts = chunk if isinstance(chunk, tuple) else (chunk,)
        split.append(len(parts))
        flat.extend(parts)
    n, nf = len(chunks), len(flat)
    has_acc = acc is not None

    def body(*refs):
        msg_refs = refs[:nf]
        kv_refs = refs[nf : nf + NY]
        pos = nf + NY
        acc_refs = refs[pos : pos + NY] if has_acc else None
        pos += NY if has_acc else 0
        dq_refs = refs[pos : pos + n]
        out_refs = refs[pos + n : pos + n + NY]
        dq_acc = refs[pos + n + NY]
        loaded, at = [], 0
        for c in range(n):
            if split[c] == 1:
                ref = msg_refs[at]
                q, g, s = ref[0:QLEN, :], ref[QLEN : 2 * QLEN, :], ref[2 * QLEN : MSG, :]
            else:
                ref = msg_refs[at + 1]
                q, g, s = msg_refs[at][...], ref[0:QLEN, :], ref[QLEN : MSG - QLEN, :]
            at += split[c]
            s = s.astype(jnp.float32)[0:1, :]
            loaded.append(
                (heads_as_rows(q), heads_as_rows(g), s[:, :ROWS] * LOG2E, s[:, ROWS:])
            )
        dq_acc[...] = jnp.zeros_like(dq_acc)
        nt = (((1,), (1,)), ((), ()))
        nn = (((1,), (0,)), ((), ()))
        tn = (((0,), (0,)), ((), ()))
        f32 = jnp.float32
        for b in range(NY):
            kv_ref = kv_refs[b]

            def step(i, carry, b=b, kv_ref=kv_ref):
                at = pl.ds(pl.multiple_of(i * TILE, TILE), TILE)
                k = kv_ref[at, 0:HD]
                v = kv_ref[at, HD : 2 * HD]
                if has_acc:
                    dk = acc_refs[b][at, 0:HD]
                    dv = acc_refs[b][at, HD : 2 * HD]
                else:
                    dk = jnp.zeros((TILE, HD), f32)
                    dv = jnp.zeros((TILE, HD), f32)
                for c in range(n):
                    q, g, total, dots = loaded[c]
                    s = lax.dot_general(k, q, nt, preferred_element_type=f32)
                    p = jnp.exp2(s * (SCALE * LOG2E) - total)
                    dp = lax.dot_general(v, g, nt, preferred_element_type=f32)
                    ds = (p * (dp - dots)).astype(jnp.bfloat16)
                    pb = p.astype(jnp.bfloat16)
                    dv = dv + lax.dot_general(pb, g, nn, preferred_element_type=f32)
                    dk = dk + lax.dot_general(ds, q, nn, preferred_element_type=f32)
                    dq_acc[c] += lax.dot_general(k, ds, tn, preferred_element_type=f32)
                if last:
                    dk = dk * SCALE
                out_refs[b][at, 0:HD] = dk.astype(out_refs[b].dtype)
                out_refs[b][at, HD : 2 * HD] = dv.astype(out_refs[b].dtype)
                return carry

            lax.fori_loop(0, BLOCK // TILE, step, 0)
        for c in range(n):
            dq_refs[c][...] = dq_acc[c].astype(jnp.bfloat16)

    out_dtypes = [jnp.float32] + [jnp.bfloat16 if last else jnp.float32] * (NY - 1)
    out_shape = [jax.ShapeDtypeStruct((HD, ROWS), jnp.bfloat16)] * n + [
        jax.ShapeDtypeStruct((BLOCK, 2 * HD), t) for t in out_dtypes
    ]
    operands = flat + list(kv) + (list(acc) if has_acc else [])
    outs = pl.pallas_call(
        body,
        out_shape=out_shape,
        scratch_shapes=[pltpu.VMEM((n, HD, ROWS), jnp.float32)],
        compiler_params=pltpu.CompilerParams(vmem_limit_bytes=VMEM),
        cost_estimate=pl.CostEstimate(
            flops=n * 10 * ROWS * NY * BLOCK * HD * 2,
            bytes_accessed=8 * 1024 * 1024,
            transcendentals=n * ROWS * NY * BLOCK,
        ),
        name="attend_%d" % n,
    )(*operands)
    return list(outs[:n]), list(outs[n:])


def dispatch_kernel(owner_ref, own_ref, a_ref, b_ref, c_ref, out_ref, sum_ref, count_ref):
    f32 = jnp.float32
    total = own_ref[...] + a_ref[...].astype(f32) + b_ref[...].astype(f32) + c_ref[...].astype(f32)
    sum_ref[...] = total.astype(jnp.bfloat16)
    out_ref[...] = jnp.zeros_like(out_ref)
    for j in range(N_VID):
        count_ref[j] = 0

    def place(f, carry):
        owner = owner_ref[f]
        slot = count_ref[owner]
        count_ref[owner] = slot + 1
        to = pl.multiple_of((owner * MOST + slot) * TPF, TPF)
        fr = pl.multiple_of(f * TPF, TPF)
        out_ref[pl.ds(to, TPF), :] = sum_ref[pl.ds(fr, TPF), :]
        return carry

    lax.fori_loop(0, FPD, place, 0)


def dispatch(owners, own, others):
    vm = pl.BlockSpec(memory_space=pltpu.VMEM)
    return pl.pallas_call(
        dispatch_kernel,
        out_shape=jax.ShapeDtypeStruct((SLOT_ROWS, 2 * HD), jnp.bfloat16),
        in_specs=[pl.BlockSpec(memory_space=pltpu.SMEM)] + [vm] * 4,
        out_specs=vm,
        scratch_shapes=[pltpu.VMEM((BLOCK, 2 * HD), jnp.bfloat16), pltpu.SMEM((N_VID,), jnp.int32)],
        compiler_params=pltpu.CompilerParams(vmem_limit_bytes=VMEM),
        name="dispatch",
    )(owners, own, *others)


def project(pieces, heads, key_weight, value_weight):
    flat, split = [], []
    for piece in pieces:
        parts = piece if isinstance(piece, tuple) else (piece,)
        split.append(len(parts))
        flat.extend(parts)
    nf = len(flat)
    cols = key_weight.shape[0]
    tile = 256

    def body(head_ref, *refs):
        piece_refs = refs[:nf]
        wk_ref, wv_ref, out_ref, w_ref = refs[nf : nf + 4]
        for p in range(KVH):
            at = pl.ds(pl.multiple_of(head_ref[p] * HD, HD), HD)
            w_ref[:, 2 * p * HD : (2 * p + 1) * HD] = wk_ref[:, at]
            w_ref[:, (2 * p + 1) * HD : (2 * p + 2) * HD] = wv_ref[:, at]
        for t in range(SLOT_ROWS // tile):
            rows, at = [], 0
            for p in range(KVH):
                if split[p] == 1:
                    rows.append(piece_refs[at][t * tile : (t + 1) * tile, :])
                else:
                    half = SLOT_ROWS // 2
                    ref = piece_refs[at + (t * tile) // half]
                    lo = (t * tile) % half
                    rows.append(ref[lo : lo + tile, :])
                at += split[p]
            a = jnp.concatenate(rows, axis=1)
            out = lax.dot_general(
                a, w_ref[...], (((1,), (1,)), ((), ())), preferred_element_type=jnp.float32
            )
            out_ref[t * tile : (t + 1) * tile, :] = out.astype(jnp.bfloat16)

    vm = pl.BlockSpec(memory_space=pltpu.VMEM)
    return pl.pallas_call(
        body,
        out_shape=jax.ShapeDtypeStruct((SLOT_ROWS, cols), jnp.bfloat16),
        in_specs=[pl.BlockSpec(memory_space=pltpu.SMEM)] + [vm] * (nf + 2),
        out_specs=vm,
        scratch_shapes=[pltpu.VMEM((cols, 2 * KVH * HD), jnp.bfloat16)],
        compiler_params=pltpu.CompilerParams(vmem_limit_bytes=VMEM),
        name="project",
    )(heads, *flat, key_weight, value_weight)


def finish_kernel(*refs):
    out_ref = refs[-1]
    total = refs[0][...].astype(jnp.float32)
    for ref in refs[1:-1]:
        total = total + ref[...].astype(jnp.float32)
    total = (total * SCALE).T
    for h in range(GROUP):
        out_ref[:, h * HD : (h + 1) * HD] = total[h * QLEN : (h + 1) * QLEN, :].astype(jnp.bfloat16)


def finish(parts):
    return pl.pallas_call(
        finish_kernel,
        out_shape=jax.ShapeDtypeStruct((QLEN, GROUP * HD), jnp.bfloat16),
        compiler_params=pltpu.CompilerParams(vmem_limit_bytes=VMEM),
        name="finish",
    )(*parts)


def on_device(
    queries,
    out_grad,
    log_totals,
    out_dots,
    lengths,
    vis_keys,
    vis_values,
    key_weight,
    value_weight,
    frame_owner,
):
    vid = lax.axis_index("vid")
    head = lax.axis_index("head")
    x, core = head // 2, head % 2

    live = jnp.arange(QLEN, dtype=jnp.int32) < lax.dynamic_index_in_dim(lengths, vid, 0, False)
    totals = jnp.where(live[None, :], log_totals, jnp.bfloat16(DEAD))
    stats = jnp.concatenate([totals.reshape(1, ROWS), out_dots.reshape(1, ROWS)], axis=1)
    msg = pl.pallas_call(
        pack_kernel, out_shape=jax.ShapeDtypeStruct((MSG, GROUP * HD), jnp.bfloat16), name="pack"
    )(queries, out_grad, stats)
    kv0 = jnp.concatenate([vis_keys, vis_values], axis=1)

    kv_up, kv_down = shift_y(kv0, 1), shift_y(kv0, -1)
    up1, down1 = shift_z(msg, 1), shift_z(msg, -1)
    half = BLOCK // 2
    far_lo, far_hi = shift_y(kv_up[:half], 1), shift_y(kv_down[half:], -1)
    kv = (kv0, kv_up, kv_down, jnp.concatenate([far_lo, far_hi], axis=0))
    up2, down2 = shift_z(up1, 1), shift_z(down1, -1)
    up3, down3 = shift_z(up2, 1), shift_z(down2, -1)
    far = (shift_z(up3[:QLEN], 1), shift_z(down3[QLEN:], -1))

    (dq0, dq_u1, dq_d1), acc = attend([msg, up1, down1], kv, None, False)
    (dq_u2, dq_d2), acc = attend([up2, down2], kv, acc, False)
    (dq_u3, dq_d3, dq_far), acc = attend([up3, down3, far], kv, acc, True)

    own, part_up, part_down, part_far = acc
    back = (shift_y(part_up, -1), shift_y(part_down, 1), shift_y(part_far, 2))
    owners = lax.dynamic_slice_in_dim(frame_owner[:, 0], vid * FPD, FPD)
    outgoing = dispatch(owners, own, back)
    mine = lax.all_to_all(outgoing, "vid", split_axis=0, concat_axis=0, tiled=True)

    r1, l1 = shift_x(mine, 1), shift_x(mine, -1)
    rows = SLOT_ROWS // 2
    r2, l2 = shift_x(r1[:rows], 1), shift_x(l1[rows:], -1)
    pieces = [mine, r1, l1, (r2, l2)]
    pieces += [swap_core(mine), swap_core(r1), swap_core(l1), (swap_core(r2), swap_core(l2))]
    xs = jnp.stack([x, (x - 1) % NX, (x + 1) % NX, (x + 2) % NX])
    heads = jnp.concatenate([xs * 2 + core, xs * 2 + 1 - core]).astype(jnp.int32)
    owned = project(pieces, heads, key_weight, value_weight)

    query_grad = finish(
        [
            dq0,
            shift_z(dq_u1, -1),
            shift_z(dq_d1, 1),
            shift_z(dq_u2, -2),
            shift_z(dq_d2, 2),
            shift_z(dq_u3, -3),
            shift_z(dq_d3, 3),
            shift_z(dq_far, 4),
        ]
    )
    return query_grad, owned


def solution(mesh):
    in_specs = (
        P("vid", "head"),
        P("vid", "head"),
        P("head", "vid"),
        P("head", "vid"),
        P(),
        P("vid", "head"),
        P("vid", "head"),
        P("head", None),
        P("head", None),
        P(),
    )
    out_specs = (P("vid", "head"), P("vid", "head"))
    return jax.shard_map(
        on_device, mesh=mesh, in_specs=in_specs, out_specs=out_specs, check_vma=False
    )
```

```python
import math

import jax
import jax.numpy as jnp
from jax import lax
from jax.experimental import pallas as pl
from jax.experimental.pallas import tpu as pltpu
from jax.sharding import PartitionSpec as P

QH = 64
KVH = 8
HD = 128
TPF = 16
QLEN = 64
GROUP = QH // KVH
ROWS = GROUP * QLEN
NZ = 8
NY = 4
NX = 4
BLOCK = 512
MSG = 2 * QLEN + 16
FPD = 32
MOST = 2
N_VID = NZ * NY
SLOT_ROWS = N_VID * MOST * TPF
SCALE = HD ** (-0.5)
LOG2E = math.log2(math.e)
DEAD = 1e30
ORDER = (0, -1, 1, -2, 2, -3, 3, 4)
EVEN = (0, 2, -2, 4)
ODD = (-1, 1, -3, 3)
VMEM = 20 * 1024 * 1024
SMALL = 8 * 1024 * 1024
MIDDLE = 12 * 1024 * 1024


def shift(a, axis, k):
    n = lax.axis_size(axis)
    return lax.ppermute(a, axis, [(i, (i + k) % n) for i in range(n)])


def run_copies(pairs, sems):
    copies = [pltpu.make_async_copy(src, dst, sems.at[i]) for i, (src, dst) in enumerate(pairs)]
    for copy in copies:
        copy.start()
    return copies


def pack_kernel(
    where_ref, len_ref, q_ref, g_ref, total_ref, dot_ref, k_ref, v_ref, msg_ref, kv_ref,
    len_at, total_at, dot_at, sems,
):
    f32 = jnp.float32
    copies = run_copies(
        [
            (len_ref, len_at),
            (total_ref, total_at),
            (dot_ref, dot_at),
            (q_ref, msg_ref.at[0:QLEN, :]),
            (g_ref, msg_ref.at[QLEN : 2 * QLEN, :]),
            (k_ref, kv_ref.at[:, 0:HD]),
            (v_ref, kv_ref.at[:, HD : 2 * HD]),
        ],
        sems,
    )
    for copy in copies[:3]:
        copy.wait()
    row = lax.broadcasted_iota(jnp.int32, (GROUP, QLEN), 1)
    total = jnp.where(row < len_at[where_ref[0]], total_at[...].astype(f32), DEAD)
    dots = dot_at[...].astype(f32)
    line = [total[h : h + 1, :] for h in range(GROUP)] + [dots[h : h + 1, :] for h in range(GROUP)]
    line = jnp.concatenate(line, axis=1)
    msg_ref[2 * QLEN :, :] = jnp.broadcast_to(line, (MSG - 2 * QLEN, 2 * ROWS)).astype(jnp.bfloat16)
    for copy in copies[3:]:
        copy.wait()


def pack(where, lengths, queries, out_grad, log_totals, out_dots, vis_keys, vis_values):
    vm = pl.BlockSpec(memory_space=pltpu.VMEM)
    sm = pl.BlockSpec(memory_space=pltpu.SMEM)
    hbm = pl.BlockSpec(memory_space=pltpu.HBM)
    return pl.pallas_call(
        pack_kernel,
        out_shape=[
            jax.ShapeDtypeStruct((MSG, GROUP * HD), jnp.bfloat16),
            jax.ShapeDtypeStruct((BLOCK, 2 * HD), jnp.bfloat16),
        ],
        in_specs=[sm] + [hbm] * 7,
        out_specs=[vm, vm],
        scratch_shapes=[
            pltpu.SMEM(lengths.shape, jnp.int32),
            pltpu.VMEM((GROUP, QLEN), jnp.bfloat16),
            pltpu.VMEM((GROUP, QLEN), jnp.bfloat16),
            pltpu.SemaphoreType.DMA((7,)),
        ],
        cost_estimate=pl.CostEstimate(flops=0, bytes_accessed=1 << 20, transcendentals=0),
        name="pack",
    )(where, lengths, queries, out_grad, log_totals, out_dots, vis_keys, vis_values)


def heads_as_rows(block):
    return jnp.concatenate([block[:, h * HD : (h + 1) * HD] for h in range(GROUP)], axis=0)


NT = (((1,), (1,)), ((), ()))
NN = (((1,), (0,)), ((), ()))
TN = (((0,), (0,)), ((), ()))


def dot32(a, b, contract):
    return lax.dot_general(a, b, contract, preferred_element_type=jnp.float32)


def load_message(ref, c, q_at, g_at, stat_at):
    rows = slice(c * ROWS, (c + 1) * ROWS)
    q_at[rows, :] = heads_as_rows(ref[0:QLEN, :])
    g_at[rows, :] = heads_as_rows(ref[QLEN : 2 * QLEN, :])
    stats = ref[2 * QLEN : MSG, :].astype(jnp.float32)[0:8, :]
    stat_at[8 * c : 8 * c + 8, 0:ROWS] = stats[:, :ROWS] * LOG2E
    stat_at[8 * c : 8 * c + 8, ROWS:] = stats[:, ROWS:]


def attend_tile(c, b, q_at, g_at, stat_at, kv, kv_acc, dq_at):
    rows = pl.ds(pl.multiple_of(c * ROWS, ROWS), ROWS)
    block = pl.ds(pl.multiple_of(b * BLOCK, BLOCK), BLOCK)
    q, g = q_at[rows, :], g_at[rows, :]
    stat = pl.ds(pl.multiple_of(c * 8, 8), 8)
    total, dots = stat_at[stat, 0:ROWS][0:1, :], stat_at[stat, ROWS:][0:1, :]
    k, v = kv[block, 0:HD], kv[block, HD : 2 * HD]
    p = jnp.exp2(dot32(k, q, NT) * (SCALE * LOG2E) - total)
    ds = (p * (dot32(v, g, NT) - dots)).astype(jnp.bfloat16)
    kv_acc[block, HD : 2 * HD] += dot32(p.astype(jnp.bfloat16), g, NN)
    kv_acc[block, 0:HD] += dot32(ds, q, NN)
    dq = pl.ds(pl.multiple_of(c * HD, HD), HD)
    dq_at[dq, :] += dot32(k, ds, TN)


def message_scratch(n):
    return [
        pltpu.VMEM((n * ROWS, HD), jnp.bfloat16),
        pltpu.VMEM((n * ROWS, HD), jnp.bfloat16),
        pltpu.VMEM((8 * n, 2 * ROWS), jnp.float32),
    ]


def attend(name, messages, blocks, accs, dqs, dq_type, acc_type, final, odd=None):
    n, nb = len(messages), len(blocks)
    in_acc = [a for a in accs if a is not None]
    in_dq = [a for a in dqs if a is not None]
    in_odd = list(odd) if odd else []
    operands = list(messages) + list(blocks) + in_acc + in_dq + in_odd
    n_in = len(operands)
    n_dq = 1 if odd else n

    def body(*refs):
        ins = list(refs[:n_in])
        dq_refs = refs[n_in : n_in + n_dq]
        out_refs = refs[n_in + n_dq : n_in + n_dq + nb]
        q_at, g_at, stat_at, kv_at, acc_at, dq_at = refs[n_in + n_dq + nb :]
        take = lambda count: [ins.pop(0) for _ in range(count)]
        msg_refs, kv_refs = take(n), take(nb)
        acc_refs = [take(1)[0] if a is not None else None for a in accs]
        dq_ins = [take(1)[0] if a is not None else None for a in dqs]
        for b in range(nb):
            block = slice(b * BLOCK, (b + 1) * BLOCK)
            kv_at[block, :] = kv_refs[b][...]
            if acc_refs[b] is None:
                acc_at[block, :] = jnp.zeros((BLOCK, 2 * HD), jnp.float32)
            else:
                acc_at[block, :] = acc_refs[b][...]
        for c in range(n):
            load_message(msg_refs[c], c, q_at, g_at, stat_at)
            rows = slice(c * HD, (c + 1) * HD)
            if dq_ins[c] is None:
                dq_at[rows, :] = jnp.zeros((HD, ROWS), jnp.float32)
            else:
                dq_at[rows, :] = dq_ins[c][...]

        def step(b, carry):
            for c in range(n):
                attend_tile(c, b, q_at, g_at, stat_at, kv_at, acc_at, dq_at)
            return carry

        if n == 1 or nb == 1:
            for b in range(nb):
                step(b, 0)
        else:
            lax.fori_loop(0, nb, step, 0)
        if odd:
            for c, ref in enumerate(ins):
                dq_refs[0][c * HD : (c + 1) * HD, :] = ref[...]
            dq_refs[0][len(ins) * HD :, :] = dq_at[...].astype(dq_type)
        else:
            for c in range(n):
                dq_refs[c][...] = dq_at[c * HD : (c + 1) * HD, :].astype(dq_type[c])
        for b in range(nb):
            block = slice(b * BLOCK, (b + 1) * BLOCK)
            dk, dv = acc_at[block, 0:HD], acc_at[block, HD : 2 * HD]
            if final:
                dk = dk * SCALE
            out_refs[b][:, 0:HD] = dk.astype(acc_type)
            out_refs[b][:, HD : 2 * HD] = dv.astype(acc_type)

    if odd:
        out_shape = [jax.ShapeDtypeStruct(((len(in_odd) + n) * HD, ROWS), dq_type)]
    else:
        out_shape = [jax.ShapeDtypeStruct((HD, ROWS), t) for t in dq_type]
    out_shape += [jax.ShapeDtypeStruct((BLOCK, 2 * HD), acc_type)] * nb
    outs = pl.pallas_call(
        body,
        out_shape=out_shape,
        scratch_shapes=message_scratch(n)
        + [
            pltpu.VMEM((nb * BLOCK, 2 * HD), jnp.bfloat16),
            pltpu.VMEM((nb * BLOCK, 2 * HD), jnp.float32),
            pltpu.VMEM((n * HD, ROWS), jnp.float32),
        ],
        compiler_params=pltpu.CompilerParams(vmem_limit_bytes=VMEM),
        cost_estimate=pl.CostEstimate(
            flops=n * 20 * ROWS * nb * BLOCK * HD,
            bytes_accessed=2 << 20,
            transcendentals=n * ROWS * nb * BLOCK,
        ),
        name=name,
    )(*operands)
    return list(outs[:n_dq]), list(outs[n_dq:])


def pair_kernel(where_ref, got_ref, *refs):
    even_refs, keep_ref, send_refs = refs[: len(EVEN)], refs[len(EVEN)], refs[len(EVEN) + 1 :]
    away = 1 - 2 * ((where_ref[0] // NY) % 2)
    for i, offset in enumerate(EVEN):
        there = (offset - away + NZ) % NZ
        slot = jnp.int32(0)
        for j, odd in enumerate(ODD):
            slot = jnp.where(there == odd % NZ, j, slot)
        got = got_ref[pl.ds(pl.multiple_of(slot * HD, HD), HD), :].astype(jnp.float32)
        total = even_refs[i][...] + got
        if i == 0:
            keep_ref[...] = total
        else:
            send_refs[i - 1][...] = total.astype(jnp.bfloat16)


def pair(where, even, got):
    vm = pl.BlockSpec(memory_space=pltpu.VMEM)
    return pl.pallas_call(
        pair_kernel,
        out_shape=[jax.ShapeDtypeStruct((HD, ROWS), jnp.float32)]
        + [jax.ShapeDtypeStruct((HD, ROWS), jnp.bfloat16)] * 3,
        in_specs=[pl.BlockSpec(memory_space=pltpu.SMEM)] + [vm] * 5,
        out_specs=[vm] * 4,
        compiler_params=pltpu.CompilerParams(vmem_limit_bytes=SMALL),
        cost_estimate=pl.CostEstimate(flops=0, bytes_accessed=2 << 20, transcendentals=0),
        name="pair",
    )(where, got, *even)


def dispatch_kernel(where_ref, owner_ref, own_ref, a_ref, b_ref, c_ref, out_ref, sum_ref, count_ref):
    f32 = jnp.float32
    total = own_ref[...] + a_ref[...].astype(f32) + b_ref[...].astype(f32) + c_ref[...].astype(f32)
    sum_ref[...] = total.astype(jnp.bfloat16)
    out_ref[...] = jnp.zeros_like(out_ref)
    for j in range(N_VID):
        count_ref[j] = 0

    def place(f, carry):
        owner = owner_ref[where_ref[0] * FPD + f]
        slot = count_ref[owner]
        count_ref[owner] = slot + 1
        to = pl.multiple_of((owner * MOST + slot) * TPF, TPF)
        fr = pl.multiple_of(f * TPF, TPF)
        out_ref[pl.ds(to, TPF), :] = sum_ref[pl.ds(fr, TPF), :]
        return carry

    lax.fori_loop(0, FPD, place, 0)


def dispatch(where, owners, own, others):
    vm = pl.BlockSpec(memory_space=pltpu.VMEM)
    return pl.pallas_call(
        dispatch_kernel,
        out_shape=jax.ShapeDtypeStruct((SLOT_ROWS, 2 * HD), jnp.bfloat16),
        in_specs=[pl.BlockSpec(memory_space=pltpu.SMEM)] * 2 + [vm] * 4,
        out_specs=vm,
        scratch_shapes=[pltpu.VMEM((BLOCK, 2 * HD), jnp.bfloat16), pltpu.SMEM((N_VID,), jnp.int32)],
        compiler_params=pltpu.CompilerParams(vmem_limit_bytes=SMALL),
        cost_estimate=pl.CostEstimate(flops=0, bytes_accessed=2 << 20, transcendentals=0),
        name="dispatch",
    )(where, owners, own, *others)


PIECES = [(dx, other) for dx in (0, -1, 1, 2) for other in (False, True)]


def project_first(head, rows, key_weight, value_weight):
    cols = key_weight.shape[0]
    feats = KVH * HD
    tile = 512

    def body(head_ref, a_ref, b_ref, wk_ref, wv_ref, acc_ref, w_ref):
        x, core = head_ref[0] // 2, head_ref[0] % 2
        for p, (dx, other) in enumerate(PIECES):
            h = ((x + dx) % NX) * 2 + (1 - core if other else core)
            at = pl.ds(pl.multiple_of(h * HD, HD), HD)
            w_ref[:, 2 * p * HD : (2 * p + 1) * HD] = wk_ref[:, at]
            w_ref[:, (2 * p + 1) * HD : (2 * p + 2) * HD] = wv_ref[:, at]
        for t in range(SLOT_ROWS // tile):
            at = slice(t * tile, (t + 1) * tile)
            a = jnp.concatenate([a_ref[at, :], b_ref[at, :]], axis=1)
            acc_ref[at, :] = dot32(a, w_ref[:, 0 : 4 * HD], NT)

    vm = pl.BlockSpec(memory_space=pltpu.VMEM)
    return pl.pallas_call(
        body,
        out_shape=[
            jax.ShapeDtypeStruct((SLOT_ROWS, cols), jnp.float32),
            jax.ShapeDtypeStruct((cols, 2 * feats), jnp.bfloat16),
        ],
        in_specs=[pl.BlockSpec(memory_space=pltpu.SMEM)] + [vm] * 4,
        out_specs=[vm, vm],
        compiler_params=pltpu.CompilerParams(vmem_limit_bytes=SMALL),
        cost_estimate=pl.CostEstimate(
            flops=SLOT_ROWS * cols * feats, bytes_accessed=10 << 20, transcendentals=0
        ),
        name="project_first",
    )(head, *rows, key_weight, value_weight)


def project_rest(acc, rows, weight):
    cols = weight.shape[0]
    tile = 512

    def body(*refs):
        acc_ref, w_ref, out_ref = refs[len(rows) :]
        for t in range(SLOT_ROWS // tile):
            at = slice(t * tile, (t + 1) * tile)
            a = jnp.concatenate([ref[at, :] for ref in refs[: len(rows)]], axis=1)
            out = acc_ref[at, :] + dot32(a, w_ref[:, 4 * HD :], NT)
            out_ref[at, :] = out.astype(jnp.bfloat16)

    return pl.pallas_call(
        body,
        out_shape=jax.ShapeDtypeStruct((SLOT_ROWS, cols), jnp.bfloat16),
        compiler_params=pltpu.CompilerParams(vmem_limit_bytes=MIDDLE),
        cost_estimate=pl.CostEstimate(
            flops=3 * SLOT_ROWS * cols * KVH * HD, bytes_accessed=10 << 20, transcendentals=0
        ),
        name="project_rest",
    )(*rows, acc, weight)


def finish_kernel(keep_ref, a_ref, b_ref, c_ref, out_ref):
    total = keep_ref[...]
    for ref in (a_ref, b_ref, c_ref):
        total = total + ref[...].astype(jnp.float32)
    total = (total * SCALE).T
    for h in range(GROUP):
        out_ref[:, h * HD : (h + 1) * HD] = total[h * QLEN : (h + 1) * QLEN, :].astype(jnp.bfloat16)


def finish(keep, others):
    return pl.pallas_call(
        finish_kernel,
        out_shape=jax.ShapeDtypeStruct((QLEN, GROUP * HD), jnp.bfloat16),
        compiler_params=pltpu.CompilerParams(vmem_limit_bytes=SMALL),
        cost_estimate=pl.CostEstimate(flops=0, bytes_accessed=1 << 19, transcendentals=0),
        name="finish",
    )(keep, *others)


def on_device(
    queries,
    out_grad,
    log_totals,
    out_dots,
    lengths,
    vis_keys,
    vis_values,
    key_weight,
    value_weight,
    frame_owner,
):
    vid = lax.axis_index("z") * NY + lax.axis_index("y")
    head = lax.axis_index("x") * 2 + lax.axis_index("core")
    where, head = vid.reshape(1), head.reshape(1)

    msg, kv0 = pack(
        where, lengths, queries, out_grad, log_totals, out_dots, vis_keys, vis_values
    )

    kv_up, kv_down = shift(kv0, "y", 1), shift(kv0, "y", -1)
    up1, down1 = shift(msg, "z", 1), shift(msg, "z", -1)
    away = [kv_up, kv_down, shift(kv0, "y", 2)]
    up2, down2 = shift(up1, "z", 1), shift(down1, "z", -1)
    bf16, f32 = jnp.bfloat16, jnp.float32
    none = [None] * NY

    near = [msg, up1, down1]
    dq, (own,) = attend("home_first", near, [kv0], none[:1], none[:3], [f32] * 3, f32, False)
    up2, down2, own = lax.optimization_barrier((up2, down2, own))
    up3, down3 = shift(up2, "z", 1), shift(down2, "z", -1)
    dq, acc = attend("away_near", near, away, none[:3], dq, [f32, bf16, bf16], f32, False)
    dq_0, dq_u1, dq_d1 = dq
    up3, down3, dq_0 = lax.optimization_barrier((up3, down3, dq_0))
    far = shift(up3, "z", 1)
    two = [up2, down2]
    (dq_u2, dq_d2), acc = attend("away_two", two, away, acc, none[:2], [f32] * 2, f32, False)
    three = [up3, down3]
    (odd,), acc = attend(
        "all_three", three, away + [kv0], acc + [own], none[:2], bf16, f32, False, (dq_u1, dq_d1)
    )
    own = acc.pop()
    (dq_4,), parts = attend("away_far", [far], away, acc, none[:1], [f32], bf16, True)

    part_up, part_down, part_far = parts
    back = (shift(part_far, "y", 2), shift(part_up, "y", -1), shift(part_down, "y", 1))
    got = lax.ppermute(odd, "z", [(i, i ^ 1) for i in range(NZ)])
    dq, (own,) = attend(
        "home_last", two + [far], [kv0], [own], [dq_u2, dq_d2, dq_4], [f32] * 3, f32, True
    )
    even = [dq_0, dq[1], dq[0], dq[2]]

    keep, *sends = pair(where, even, got)
    others = [shift(rows, "z", offset) for rows, offset in zip(sends, EVEN[1:])]
    own, keep = lax.optimization_barrier((own, keep))

    outgoing = dispatch(where, frame_owner.reshape(-1), own, back)
    mine = lax.all_to_all(outgoing, ("z", "y"), split_axis=0, concat_axis=0, tiled=True)
    mine, *others = lax.optimization_barrier((mine, *others))

    right, left, across = shift(mine, "x", 1), shift(mine, "x", -1), shift(mine, "x", 2)
    here = [mine, shift(mine, "core", 1)]
    acc, weight = project_first(head, here, key_weight, value_weight)
    query_grad = finish(keep, others)
    pieces = []
    for rows in (right, left, across):
        pieces += [rows, shift(rows, "core", 1)]
    acc, query_grad = lax.optimization_barrier((acc, query_grad))
    return query_grad, project_rest(acc, pieces, weight)


def solution(mesh):
    devices = mesh.devices.reshape(NZ, NY, NX, 2)
    split = jax.sharding.Mesh(devices, ("z", "y", "x", "core"))
    vid, head = ("z", "y"), ("x", "core")
    in_specs = (
        P(vid, head),
        P(vid, head),
        P(head, vid),
        P(head, vid),
        P(),
        P(vid, head),
        P(vid, head),
        P(head, None),
        P(head, None),
        P(),
    )
    out_specs = (P(vid, head), P(vid, head))
    return jax.shard_map(
        on_device, mesh=split, in_specs=in_specs, out_specs=out_specs, check_vma=False
    )
```

```python
import math

import jax
import jax.numpy as jnp
from jax import lax
from jax.experimental import pallas as pl
from jax.experimental.pallas import tpu as pltpu
from jax.sharding import PartitionSpec as P

QH = 64
KVH = 8
HD = 128
TPF = 16
QLEN = 64
GROUP = QH // KVH
ROWS = GROUP * QLEN
NZ = 8
NY = 4
NX = 4
Z = ("zq", "zp")
BLOCK = 512
MSG = 2 * QLEN + 16
FPD = 32
MOST = 2
N_VID = NZ * NY
SLOT_ROWS = N_VID * MOST * TPF
SCALE = HD ** (-0.5)
LOG2E = math.log2(math.e)
DEAD = 1e30
ORDER = (0, -1, 1, -2, 2, -3, 3, 4)
EVEN = (0, 2, -2, 4)
ODD = (-1, 1, -3, 3)
VMEM = 20 * 1024 * 1024
SMALL = 8 * 1024 * 1024
MIDDLE = 12 * 1024 * 1024


SIZES = {"z": NZ, "y": NY, "x": NX, "core": 2}


def shift(a, axis, k):
    n = SIZES[axis]
    return lax.ppermute(a, Z if axis == "z" else axis, [(i, (i + k) % n) for i in range(n)])


def shift_by_core(a, k):
    pairs = []
    for x in range(NX):
        for core, by in ((0, k), (1, -k)):
            pairs.append((2 * x + core, 2 * ((x + by) % NX) + core))
    return lax.ppermute(a, ("x", "core"), pairs)


def run_copies(pairs, sems):
    copies = [pltpu.make_async_copy(src, dst, sems.at[i]) for i, (src, dst) in enumerate(pairs)]
    for copy in copies:
        copy.start()
    return copies


def pack_kernel(
    where_ref, len_ref, q_ref, g_ref, total_ref, dot_ref, k_ref, v_ref, msg_ref, kv_ref,
    len_at, total_at, dot_at, sems,
):
    f32 = jnp.float32
    copies = run_copies(
        [
            (len_ref, len_at),
            (total_ref, total_at),
            (dot_ref, dot_at),
            (q_ref, msg_ref.at[0:QLEN, :]),
            (g_ref, msg_ref.at[QLEN : 2 * QLEN, :]),
            (k_ref, kv_ref.at[:, 0:HD]),
            (v_ref, kv_ref.at[:, HD : 2 * HD]),
        ],
        sems,
    )
    for copy in copies[:3]:
        copy.wait()
    row = lax.broadcasted_iota(jnp.int32, (GROUP, QLEN), 1)
    total = jnp.where(row < len_at[where_ref[0]], total_at[...].astype(f32), DEAD)
    dots = dot_at[...].astype(f32)
    line = [total[h : h + 1, :] for h in range(GROUP)] + [dots[h : h + 1, :] for h in range(GROUP)]
    line = jnp.concatenate(line, axis=1)
    msg_ref[2 * QLEN :, :] = jnp.broadcast_to(line, (MSG - 2 * QLEN, 2 * ROWS)).astype(jnp.bfloat16)
    for copy in copies[3:]:
        copy.wait()


def pack(where, lengths, queries, out_grad, log_totals, out_dots, vis_keys, vis_values):
    vm = pl.BlockSpec(memory_space=pltpu.VMEM)
    sm = pl.BlockSpec(memory_space=pltpu.SMEM)
    hbm = pl.BlockSpec(memory_space=pltpu.HBM)
    return pl.pallas_call(
        pack_kernel,
        out_shape=[
            jax.ShapeDtypeStruct((MSG, GROUP * HD), jnp.bfloat16),
            jax.ShapeDtypeStruct((BLOCK, 2 * HD), jnp.bfloat16),
        ],
        in_specs=[sm] + [hbm] * 7,
        out_specs=[vm, vm],
        scratch_shapes=[
            pltpu.SMEM(lengths.shape, jnp.int32),
            pltpu.VMEM((GROUP, QLEN), jnp.bfloat16),
            pltpu.VMEM((GROUP, QLEN), jnp.bfloat16),
            pltpu.SemaphoreType.DMA((7,)),
        ],
        cost_estimate=pl.CostEstimate(flops=0, bytes_accessed=1 << 20, transcendentals=0),
        name="pack",
    )(where, lengths, queries, out_grad, log_totals, out_dots, vis_keys, vis_values)


def heads_as_rows(block):
    return jnp.concatenate([block[:, h * HD : (h + 1) * HD] for h in range(GROUP)], axis=0)


NT = (((1,), (1,)), ((), ()))
NN = (((1,), (0,)), ((), ()))
TN = (((0,), (0,)), ((), ()))


def dot32(a, b, contract):
    return lax.dot_general(a, b, contract, preferred_element_type=jnp.float32)


def load_message(ref, c, q_at, g_at, stat_at):
    rows = slice(c * ROWS, (c + 1) * ROWS)
    q_at[rows, :] = heads_as_rows(ref[0:QLEN, :])
    g_at[rows, :] = heads_as_rows(ref[QLEN : 2 * QLEN, :])
    stats = ref[2 * QLEN : MSG, :].astype(jnp.float32)[0:8, :]
    stat_at[8 * c : 8 * c + 8, 0:ROWS] = stats[:, :ROWS] * LOG2E
    stat_at[8 * c : 8 * c + 8, ROWS:] = stats[:, ROWS:]


def attend_tile(c, b, q_at, g_at, stat_at, kv, kv_acc, dq_at):
    rows = pl.ds(pl.multiple_of(c * ROWS, ROWS), ROWS)
    block = pl.ds(pl.multiple_of(b * BLOCK, BLOCK), BLOCK)
    q, g = q_at[rows, :], g_at[rows, :]
    stat = pl.ds(pl.multiple_of(c * 8, 8), 8)
    total, dots = stat_at[stat, 0:ROWS][0:1, :], stat_at[stat, ROWS:][0:1, :]
    k, v = kv[block, 0:HD], kv[block, HD : 2 * HD]
    p = jnp.exp2(dot32(k, q, NT) * (SCALE * LOG2E) - total)
    ds = (p * (dot32(v, g, NT) - dots)).astype(jnp.bfloat16)
    kv_acc[block, HD : 2 * HD] += dot32(p.astype(jnp.bfloat16), g, NN)
    kv_acc[block, 0:HD] += dot32(ds, q, NN)
    dq = pl.ds(pl.multiple_of(c * HD, HD), HD)
    dq_at[dq, :] += dot32(k, ds, TN)


def message_scratch(n):
    return [
        pltpu.VMEM((n * ROWS, HD), jnp.bfloat16),
        pltpu.VMEM((n * ROWS, HD), jnp.bfloat16),
        pltpu.VMEM((8 * n, 2 * ROWS), jnp.float32),
    ]


def attend(name, messages, blocks, accs, dqs, dq_type, acc_type, final, odd=None):
    n, nb = len(messages), len(blocks)
    in_acc = [a for a in accs if a is not None]
    in_dq = [a for a in dqs if a is not None]
    in_odd = list(odd) if odd else []
    operands = list(messages) + list(blocks) + in_acc + in_dq + in_odd
    n_in = len(operands)
    n_dq = 1 if odd else n

    def body(*refs):
        ins = list(refs[:n_in])
        dq_refs = refs[n_in : n_in + n_dq]
        out_refs = refs[n_in + n_dq : n_in + n_dq + nb]
        q_at, g_at, stat_at, kv_at, acc_at, dq_at = refs[n_in + n_dq + nb :]
        take = lambda count: [ins.pop(0) for _ in range(count)]
        msg_refs, kv_refs = take(n), take(nb)
        acc_refs = [take(1)[0] if a is not None else None for a in accs]
        dq_ins = [take(1)[0] if a is not None else None for a in dqs]
        for b in range(nb):
            block = slice(b * BLOCK, (b + 1) * BLOCK)
            kv_at[block, :] = kv_refs[b][...]
            if acc_refs[b] is None:
                acc_at[block, :] = jnp.zeros((BLOCK, 2 * HD), jnp.float32)
            else:
                acc_at[block, :] = acc_refs[b][...]
        for c in range(n):
            load_message(msg_refs[c], c, q_at, g_at, stat_at)
            rows = slice(c * HD, (c + 1) * HD)
            if dq_ins[c] is None:
                dq_at[rows, :] = jnp.zeros((HD, ROWS), jnp.float32)
            else:
                dq_at[rows, :] = dq_ins[c][...]

        def step(b, carry):
            for c in range(n):
                attend_tile(c, b, q_at, g_at, stat_at, kv_at, acc_at, dq_at)
            return carry

        if n == 1 or nb == 1:
            for b in range(nb):
                step(b, 0)
        else:
            lax.fori_loop(0, nb, step, 0)
        if odd:
            for c, ref in enumerate(ins):
                dq_refs[0][c * HD : (c + 1) * HD, :] = ref[...]
            dq_refs[0][len(ins) * HD :, :] = dq_at[...].astype(dq_type)
        else:
            for c in range(n):
                dq_refs[c][...] = dq_at[c * HD : (c + 1) * HD, :].astype(dq_type[c])
        for b in range(nb):
            block = slice(b * BLOCK, (b + 1) * BLOCK)
            dk, dv = acc_at[block, 0:HD], acc_at[block, HD : 2 * HD]
            if final:
                dk = dk * SCALE
            out_refs[b][:, 0:HD] = dk.astype(acc_type)
            out_refs[b][:, HD : 2 * HD] = dv.astype(acc_type)

    if odd:
        out_shape = [jax.ShapeDtypeStruct(((len(in_odd) + n) * HD, ROWS), dq_type)]
    else:
        out_shape = [jax.ShapeDtypeStruct((HD, ROWS), t) for t in dq_type]
    out_shape += [jax.ShapeDtypeStruct((BLOCK, 2 * HD), acc_type)] * nb
    outs = pl.pallas_call(
        body,
        out_shape=out_shape,
        scratch_shapes=message_scratch(n)
        + [
            pltpu.VMEM((nb * BLOCK, 2 * HD), jnp.bfloat16),
            pltpu.VMEM((nb * BLOCK, 2 * HD), jnp.float32),
            pltpu.VMEM((n * HD, ROWS), jnp.float32),
        ],
        compiler_params=pltpu.CompilerParams(vmem_limit_bytes=VMEM),
        cost_estimate=pl.CostEstimate(
            flops=n * 20 * ROWS * nb * BLOCK * HD,
            bytes_accessed=2 << 20,
            transcendentals=n * ROWS * nb * BLOCK,
        ),
        name=name,
    )(*operands)
    return list(outs[:n_dq]), list(outs[n_dq:])


def pair_kernel(where_ref, got_ref, *refs):
    even_refs, out_ref = refs[: len(EVEN)], refs[len(EVEN)]
    z = where_ref[0] // NY
    away = 1 - 2 * (z % 2)
    for i, offset in enumerate(EVEN):
        there = (offset - away + NZ) % NZ
        slot = jnp.int32(0)
        for j, odd in enumerate(ODD):
            slot = jnp.where(there == odd % NZ, j, slot)
        got = got_ref[pl.ds(pl.multiple_of(slot * HD, HD), HD), :].astype(jnp.float32)
        to = ((z + offset + NZ) % NZ) // 2
        total = even_refs[i][...] + got
        out_ref[pl.ds(pl.multiple_of(to * HD, HD), HD), :] = total.astype(jnp.bfloat16)


def pair(where, even, got):
    vm = pl.BlockSpec(memory_space=pltpu.VMEM)
    return pl.pallas_call(
        pair_kernel,
        out_shape=jax.ShapeDtypeStruct((len(EVEN) * HD, ROWS), jnp.bfloat16),
        in_specs=[pl.BlockSpec(memory_space=pltpu.SMEM)] + [vm] * 5,
        out_specs=vm,
        compiler_params=pltpu.CompilerParams(vmem_limit_bytes=SMALL),
        cost_estimate=pl.CostEstimate(flops=0, bytes_accessed=2 << 20, transcendentals=0),
        name="pair",
    )(where, got, *even)


def dispatch_kernel(where_ref, owner_ref, own_ref, a_ref, b_ref, c_ref, out_ref, sum_ref, count_ref):
    f32 = jnp.float32
    total = own_ref[...] + a_ref[...].astype(f32) + b_ref[...].astype(f32) + c_ref[...].astype(f32)
    sum_ref[...] = total.astype(jnp.bfloat16)
    out_ref[...] = jnp.zeros_like(out_ref)
    for j in range(N_VID):
        count_ref[j] = 0

    def place(f, carry):
        owner = owner_ref[where_ref[0] * FPD + f]
        slot = count_ref[owner]
        count_ref[owner] = slot + 1
        to = pl.multiple_of((owner * MOST + slot) * TPF, TPF)
        fr = pl.multiple_of(f * TPF, TPF)
        out_ref[pl.ds(to, TPF), :] = sum_ref[pl.ds(fr, TPF), :]
        return carry

    lax.fori_loop(0, FPD, place, 0)


def dispatch(where, owners, own, others):
    vm = pl.BlockSpec(memory_space=pltpu.VMEM)
    return pl.pallas_call(
        dispatch_kernel,
        out_shape=jax.ShapeDtypeStruct((SLOT_ROWS, 2 * HD), jnp.bfloat16),
        in_specs=[pl.BlockSpec(memory_space=pltpu.SMEM)] * 2 + [vm] * 4,
        out_specs=vm,
        scratch_shapes=[pltpu.VMEM((BLOCK, 2 * HD), jnp.bfloat16), pltpu.SMEM((N_VID,), jnp.int32)],
        compiler_params=pltpu.CompilerParams(vmem_limit_bytes=SMALL),
        cost_estimate=pl.CostEstimate(flops=0, bytes_accessed=2 << 20, transcendentals=0),
        name="dispatch",
    )(where, owners, own, *others)


PIECES = [(dx, other) for dx in (0, -1, 1, 2) for other in (False, True)]


def merge_kernel(where_ref, wk_ref, wv_ref, out_ref):
    x, core = where_ref[1] // 2, where_ref[1] % 2
    for p, (dx, other) in enumerate(PIECES):
        by = 1 - core if other else core
        h = ((x + dx * (1 - 2 * by) + NX) % NX) * 2 + by
        at = pl.ds(pl.multiple_of(h * HD, HD), HD)
        out_ref[:, 2 * p * HD : (2 * p + 1) * HD] = wk_ref[:, at]
        out_ref[:, (2 * p + 1) * HD : (2 * p + 2) * HD] = wv_ref[:, at]


def merge(where, key_weight, value_weight):
    vm = pl.BlockSpec(memory_space=pltpu.VMEM)
    return pl.pallas_call(
        merge_kernel,
        out_shape=jax.ShapeDtypeStruct((key_weight.shape[0], 2 * KVH * HD), jnp.bfloat16),
        in_specs=[pl.BlockSpec(memory_space=pltpu.SMEM), vm, vm],
        out_specs=vm,
        compiler_params=pltpu.CompilerParams(vmem_limit_bytes=SMALL),
        cost_estimate=pl.CostEstimate(flops=0, bytes_accessed=8 << 20, transcendentals=0),
        name="merge",
    )(where, key_weight, value_weight)


def project(pieces, weight):
    cols = weight.shape[0]
    tile = 512
    n_tile = SLOT_ROWS // tile

    def body(*refs):
        w_ref, out_ref, out_at, sems = refs[KVH:]
        copies = []
        for t in range(n_tile):
            rows = slice(t * tile, (t + 1) * tile)
            a = jnp.concatenate([ref[rows, :] for ref in refs[:KVH]], axis=1)
            out_at[rows, :] = dot32(a, w_ref[...], NT).astype(jnp.bfloat16)
            copy = pltpu.make_async_copy(out_at.at[rows, :], out_ref.at[rows, :], sems.at[t])
            copy.start()
            copies.append(copy)
        for copy in copies:
            copy.wait()

    vm = pl.BlockSpec(memory_space=pltpu.VMEM)
    return pl.pallas_call(
        body,
        out_shape=jax.ShapeDtypeStruct((SLOT_ROWS, cols), jnp.bfloat16),
        in_specs=[vm] * (KVH + 1),
        out_specs=pl.BlockSpec(memory_space=pltpu.HBM),
        scratch_shapes=[
            pltpu.VMEM((SLOT_ROWS, cols), jnp.bfloat16),
            pltpu.SemaphoreType.DMA((n_tile,)),
        ],
        compiler_params=pltpu.CompilerParams(vmem_limit_bytes=MIDDLE),
        cost_estimate=pl.CostEstimate(
            flops=4 * SLOT_ROWS * cols * KVH * HD, bytes_accessed=10 << 20, transcendentals=0
        ),
        name="project",
    )(*pieces, weight)


def finish_kernel(part_ref, out_ref):
    total = part_ref[0:HD, :].astype(jnp.float32)
    for i in range(1, len(EVEN)):
        total = total + part_ref[i * HD : (i + 1) * HD, :].astype(jnp.float32)
    total = (total * SCALE).T
    for h in range(GROUP):
        out_ref[:, h * HD : (h + 1) * HD] = total[h * QLEN : (h + 1) * QLEN, :].astype(jnp.bfloat16)


def finish(parts):
    return pl.pallas_call(
        finish_kernel,
        out_shape=jax.ShapeDtypeStruct((QLEN, GROUP * HD), jnp.bfloat16),
        compiler_params=pltpu.CompilerParams(vmem_limit_bytes=SMALL),
        cost_estimate=pl.CostEstimate(flops=0, bytes_accessed=1 << 19, transcendentals=0),
        name="finish",
    )(parts)


def on_device(
    queries,
    out_grad,
    log_totals,
    out_dots,
    lengths,
    vis_keys,
    vis_values,
    key_weight,
    value_weight,
    frame_owner,
):
    vid = lax.axis_index(Z) * NY + lax.axis_index("y")
    head = lax.axis_index("x") * 2 + lax.axis_index("core")
    where = jnp.stack([vid, head])

    msg, kv0 = pack(
        where, lengths, queries, out_grad, log_totals, out_dots, vis_keys, vis_values
    )

    kv_up, kv_down = shift(kv0, "y", 1), shift(kv0, "y", -1)
    up1, down1 = shift(msg, "z", 1), shift(msg, "z", -1)
    away = [kv_up, kv_down, shift(kv0, "y", 2)]
    up2, down2 = shift(up1, "z", 1), shift(down1, "z", -1)
    bf16, f32 = jnp.bfloat16, jnp.float32
    none = [None] * NY

    near = [msg, up1, down1]
    dq, (own,) = attend("home_first", near, [kv0], none[:1], none[:3], [f32] * 3, f32, False)
    up2, down2, own = lax.optimization_barrier((up2, down2, own))
    up3, down3 = shift(up2, "z", 1), shift(down2, "z", -1)
    dq, acc = attend("away_near", near, away, none[:3], dq, [f32, bf16, bf16], f32, False)
    dq_0, dq_u1, dq_d1 = dq
    up3, down3, dq_0 = lax.optimization_barrier((up3, down3, dq_0))
    far = shift(up3, "z", 1)
    two = [up2, down2]
    (dq_u2, dq_d2), acc = attend("away_two", two, away, acc, none[:2], [f32] * 2, f32, False)
    three = [up3, down3]
    (odd,), acc = attend(
        "all_three", three, away + [kv0], acc + [own], none[:2], bf16, f32, False, (dq_u1, dq_d1)
    )
    own = acc.pop()
    (dq_4,), parts = attend("away_far", [far], away, acc, none[:1], [f32], bf16, True)

    part_up, part_down, part_far = parts
    back = (shift(part_far, "y", 2), shift(part_up, "y", -1), shift(part_down, "y", 1))
    got = lax.ppermute(odd, "zp", [(0, 1), (1, 0)])
    dq, (own,) = attend(
        "home_last", two + [far], [kv0], [own], [dq_u2, dq_d2, dq_4], [f32] * 3, f32, True
    )
    even = [dq_0, dq[1], dq[0], dq[2]]

    paired = pair(where, even, got)
    own, paired = lax.optimization_barrier((own, paired))

    outgoing = dispatch(where, frame_owner.reshape(-1), own, back)
    mine = lax.all_to_all(outgoing, Z + ("y",), split_axis=0, concat_axis=0, tiled=True)
    paired, mine = lax.optimization_barrier((paired, mine))

    first, second = shift_by_core(mine, 1), shift_by_core(mine, -1)
    pieces = [mine, shift(mine, "core", 1)]
    first, second = lax.optimization_barrier((first, second))
    across = shift_by_core(first, 1)
    for rows in (first, second):
        pieces += [rows, shift(rows, "core", 1)]
    parts = lax.all_to_all(paired, "zq", split_axis=0, concat_axis=0, tiled=True)
    query_grad = finish(parts)
    where, query_grad = lax.optimization_barrier((where, query_grad))
    weight = merge(where, key_weight, value_weight)
    across, weight = lax.optimization_barrier((across, weight))
    pieces += [across, shift(across, "core", 1)]
    return query_grad, project(pieces, weight)


def solution(mesh):
    devices = mesh.devices.reshape(NZ // 2, 2, NY, NX, 2)
    split = jax.sharding.Mesh(devices, Z + ("y", "x", "core"))
    vid, head = Z + ("y",), ("x", "core")
    in_specs = (
        P(vid, head),
        P(vid, head),
        P(head, vid),
        P(head, vid),
        P(),
        P(vid, head),
        P(vid, head),
        P(head, None),
        P(head, None),
        P(),
    )
    out_specs = (P(vid, head), P(vid, head))
    return jax.shard_map(
        on_device, mesh=split, in_specs=in_specs, out_specs=out_specs, check_vma=False
    )
```

```python
import math

import jax
import jax.numpy as jnp
from jax import lax
from jax.experimental import pallas as pl
from jax.experimental.pallas import tpu as pltpu
from jax.sharding import PartitionSpec as P

QH = 64
KVH = 8
HD = 128
TPF = 16
QLEN = 64
GROUP = QH // KVH
ROWS = GROUP * QLEN
NZ = 8
NY = 4
NX = 4
Z = ("zq", "zp")
BLOCK = 512
MSG = 2 * QLEN + 16
FPD = 32
MOST = 2
N_VID = NZ * NY
SLOT_ROWS = N_VID * MOST * TPF
SCALE = HD ** (-0.5)
LOG2E = math.log2(math.e)
DEAD = 1e30
ORDER = (0, -1, 1, -2, 2, -3, 3, 4)
EVEN = (0, 2, -2, 4)
ODD = (-1, 1, -3, 3)
VMEM = 20 * 1024 * 1024
SMALL = 8 * 1024 * 1024
MIDDLE = 12 * 1024 * 1024


SIZES = {"z": NZ, "y": NY, "x": NX, "core": 2}


def shift(a, axis, k):
    n = SIZES[axis]
    return lax.ppermute(a, Z if axis == "z" else axis, [(i, (i + k) % n) for i in range(n)])


def shift_by_core(a, k):
    pairs = []
    for x in range(NX):
        for core, by in ((0, k), (1, -k)):
            pairs.append((2 * x + core, 2 * ((x + by) % NX) + core))
    return lax.ppermute(a, ("x", "core"), pairs)


def vid_index():
    return (lax.axis_index("zq") * 2 + lax.axis_index("zp")) * NY + lax.axis_index("y")


def run_copies(pairs, sems):
    copies = [pltpu.make_async_copy(src, dst, sems.at[i]) for i, (src, dst) in enumerate(pairs)]
    for copy in copies:
        copy.start()
    return copies


def pack_kernel(
    len_ref, q_ref, g_ref, total_ref, dot_ref, k_ref, v_ref, msg_ref, kv_ref,
    len_at, total_at, dot_at, sems,
):
    f32 = jnp.float32
    copies = run_copies(
        [
            (len_ref, len_at),
            (total_ref, total_at),
            (dot_ref, dot_at),
            (q_ref, msg_ref.at[0:QLEN, :]),
            (g_ref, msg_ref.at[QLEN : 2 * QLEN, :]),
            (k_ref, kv_ref.at[:, 0:HD]),
            (v_ref, kv_ref.at[:, HD : 2 * HD]),
        ],
        sems,
    )
    for copy in copies[:3]:
        copy.wait()
    row = lax.broadcasted_iota(jnp.int32, (GROUP, QLEN), 1)
    total = jnp.where(row < len_at[vid_index()], total_at[...].astype(f32), DEAD)
    dots = dot_at[...].astype(f32)
    line = [total[h : h + 1, :] for h in range(GROUP)] + [dots[h : h + 1, :] for h in range(GROUP)]
    line = jnp.concatenate(line, axis=1)
    msg_ref[2 * QLEN :, :] = jnp.broadcast_to(line, (MSG - 2 * QLEN, 2 * ROWS)).astype(jnp.bfloat16)
    for copy in copies[3:]:
        copy.wait()


def pack(lengths, queries, out_grad, log_totals, out_dots, vis_keys, vis_values):
    vm = pl.BlockSpec(memory_space=pltpu.VMEM)
    hbm = pl.BlockSpec(memory_space=pltpu.HBM)
    return pl.pallas_call(
        pack_kernel,
        out_shape=[
            jax.ShapeDtypeStruct((MSG, GROUP * HD), jnp.bfloat16),
            jax.ShapeDtypeStruct((BLOCK, 2 * HD), jnp.bfloat16),
        ],
        in_specs=[hbm] * 7,
        out_specs=[vm, vm],
        scratch_shapes=[
            pltpu.SMEM(lengths.shape, jnp.int32),
            pltpu.VMEM((GROUP, QLEN), jnp.bfloat16),
            pltpu.VMEM((GROUP, QLEN), jnp.bfloat16),
            pltpu.SemaphoreType.DMA((7,)),
        ],
        cost_estimate=pl.CostEstimate(flops=0, bytes_accessed=1 << 20, transcendentals=0),
        name="pack",
    )(lengths, queries, out_grad, log_totals, out_dots, vis_keys, vis_values)


def heads_as_rows(block):
    return jnp.concatenate([block[:, h * HD : (h + 1) * HD] for h in range(GROUP)], axis=0)


NT = (((1,), (1,)), ((), ()))
NN = (((1,), (0,)), ((), ()))
TN = (((0,), (0,)), ((), ()))


def dot32(a, b, contract):
    return lax.dot_general(a, b, contract, preferred_element_type=jnp.float32)


def load_message(ref, c, q_at, g_at, stat_at):
    rows = slice(c * ROWS, (c + 1) * ROWS)
    q_at[rows, :] = heads_as_rows(ref[0:QLEN, :])
    g_at[rows, :] = heads_as_rows(ref[QLEN : 2 * QLEN, :])
    stats = ref[2 * QLEN : MSG, :].astype(jnp.float32)[0:8, :]
    stat_at[8 * c : 8 * c + 8, 0:ROWS] = stats[:, :ROWS] * LOG2E
    stat_at[8 * c : 8 * c + 8, ROWS:] = stats[:, ROWS:]


def attend_tile(c, b, q_at, g_at, stat_at, kv, kv_acc, dq_at):
    rows = pl.ds(pl.multiple_of(c * ROWS, ROWS), ROWS)
    block = pl.ds(pl.multiple_of(b * BLOCK, BLOCK), BLOCK)
    q, g = q_at[rows, :], g_at[rows, :]
    stat = pl.ds(pl.multiple_of(c * 8, 8), 8)
    total, dots = stat_at[stat, 0:ROWS][0:1, :], stat_at[stat, ROWS:][0:1, :]
    k, v = kv[block, 0:HD], kv[block, HD : 2 * HD]
    p = jnp.exp2(dot32(k, q, NT) * (SCALE * LOG2E) - total)
    ds = (p * (dot32(v, g, NT) - dots)).astype(jnp.bfloat16)
    kv_acc[block, HD : 2 * HD] += dot32(p.astype(jnp.bfloat16), g, NN)
    kv_acc[block, 0:HD] += dot32(ds, q, NN)
    dq = pl.ds(pl.multiple_of(c * HD, HD), HD)
    dq_at[dq, :] += dot32(k, ds, TN)


def message_scratch(n):
    return [
        pltpu.VMEM((n * ROWS, HD), jnp.bfloat16),
        pltpu.VMEM((n * ROWS, HD), jnp.bfloat16),
        pltpu.VMEM((8 * n, 2 * ROWS), jnp.float32),
    ]


def attend(name, messages, blocks, accs, dqs, dq_type, acc_type, final, odd=None):
    n, nb = len(messages), len(blocks)
    in_acc = [a for a in accs if a is not None]
    in_dq = [a for a in dqs if a is not None]
    in_odd = list(odd) if odd else []
    operands = list(messages) + list(blocks) + in_acc + in_dq + in_odd
    n_in = len(operands)
    n_dq = 1 if odd else n

    def body(*refs):
        ins = list(refs[:n_in])
        dq_refs = refs[n_in : n_in + n_dq]
        out_refs = refs[n_in + n_dq : n_in + n_dq + nb]
        q_at, g_at, stat_at, kv_at, acc_at, dq_at = refs[n_in + n_dq + nb :]
        take = lambda count: [ins.pop(0) for _ in range(count)]
        msg_refs, kv_refs = take(n), take(nb)
        acc_refs = [take(1)[0] if a is not None else None for a in accs]
        dq_ins = [take(1)[0] if a is not None else None for a in dqs]
        for b in range(nb):
            block = slice(b * BLOCK, (b + 1) * BLOCK)
            kv_at[block, :] = kv_refs[b][...]
            if acc_refs[b] is None:
                acc_at[block, :] = jnp.zeros((BLOCK, 2 * HD), jnp.float32)
            else:
                acc_at[block, :] = acc_refs[b][...]
        for c in range(n):
            load_message(msg_refs[c], c, q_at, g_at, stat_at)
            rows = slice(c * HD, (c + 1) * HD)
            if dq_ins[c] is None:
                dq_at[rows, :] = jnp.zeros((HD, ROWS), jnp.float32)
            else:
                dq_at[rows, :] = dq_ins[c][...]

        def step(b, carry):
            for c in range(n):
                attend_tile(c, b, q_at, g_at, stat_at, kv_at, acc_at, dq_at)
            return carry

        if n == 1 or nb == 1:
            for b in range(nb):
                step(b, 0)
        else:
            lax.fori_loop(0, nb, step, 0)
        if odd:
            for c, ref in enumerate(ins):
                dq_refs[0][c * HD : (c + 1) * HD, :] = ref[...]
            dq_refs[0][len(ins) * HD :, :] = dq_at[...].astype(dq_type)
        else:
            for c in range(n):
                dq_refs[c][...] = dq_at[c * HD : (c + 1) * HD, :].astype(dq_type[c])
        for b in range(nb):
            block = slice(b * BLOCK, (b + 1) * BLOCK)
            dk, dv = acc_at[block, 0:HD], acc_at[block, HD : 2 * HD]
            if final:
                dk = dk * SCALE
            out_refs[b][:, 0:HD] = dk.astype(acc_type)
            out_refs[b][:, HD : 2 * HD] = dv.astype(acc_type)

    if odd:
        out_shape = [jax.ShapeDtypeStruct(((len(in_odd) + n) * HD, ROWS), dq_type)]
    else:
        out_shape = [jax.ShapeDtypeStruct((HD, ROWS), t) for t in dq_type]
    out_shape += [jax.ShapeDtypeStruct((BLOCK, 2 * HD), acc_type)] * nb
    outs = pl.pallas_call(
        body,
        out_shape=out_shape,
        scratch_shapes=message_scratch(n)
        + [
            pltpu.VMEM((nb * BLOCK, 2 * HD), jnp.bfloat16),
            pltpu.VMEM((nb * BLOCK, 2 * HD), jnp.float32),
            pltpu.VMEM((n * HD, ROWS), jnp.float32),
        ],
        compiler_params=pltpu.CompilerParams(vmem_limit_bytes=VMEM),
        cost_estimate=pl.CostEstimate(
            flops=n * 20 * ROWS * nb * BLOCK * HD,
            bytes_accessed=2 << 20,
            transcendentals=n * ROWS * nb * BLOCK,
        ),
        name=name,
    )(*operands)
    return list(outs[:n_dq]), list(outs[n_dq:])


def pair_kernel(got_ref, *refs):
    even_refs, keep_ref, send_refs = refs[: len(EVEN)], refs[len(EVEN)], refs[len(EVEN) + 1 :]
    away = 1 - 2 * (lax.axis_index("zp"))
    for i, offset in enumerate(EVEN):
        there = (offset - away + NZ) % NZ
        slot = jnp.int32(0)
        for j, odd in enumerate(ODD):
            slot = jnp.where(there == odd % NZ, j, slot)
        got = got_ref[pl.ds(pl.multiple_of(slot * HD, HD), HD), :].astype(jnp.float32)
        total = even_refs[i][...] + got
        if i == 0:
            keep_ref[...] = total
        else:
            send_refs[i - 1][...] = total.astype(jnp.bfloat16)


def pair(even, got):
    vm = pl.BlockSpec(memory_space=pltpu.VMEM)
    return pl.pallas_call(
        pair_kernel,
        out_shape=[jax.ShapeDtypeStruct((HD, ROWS), jnp.float32)]
        + [jax.ShapeDtypeStruct((HD, ROWS), jnp.bfloat16)] * 3,
        in_specs=[vm] * 5,
        out_specs=[vm] * 4,
        compiler_params=pltpu.CompilerParams(vmem_limit_bytes=SMALL),
        cost_estimate=pl.CostEstimate(flops=0, bytes_accessed=2 << 20, transcendentals=0),
        name="pair",
    )(got, *even)


def dispatch_kernel(owner_ref, own_ref, a_ref, b_ref, c_ref, out_ref, sum_ref, count_ref):
    f32 = jnp.float32
    total = own_ref[...] + a_ref[...].astype(f32) + b_ref[...].astype(f32) + c_ref[...].astype(f32)
    sum_ref[...] = total.astype(jnp.bfloat16)
    out_ref[...] = jnp.zeros_like(out_ref)
    for j in range(N_VID):
        count_ref[j] = 0

    first = vid_index() * FPD

    def place(f, carry):
        owner = owner_ref[first + f]
        slot = count_ref[owner]
        count_ref[owner] = slot + 1
        to = pl.multiple_of((owner * MOST + slot) * TPF, TPF)
        fr = pl.multiple_of(f * TPF, TPF)
        out_ref[pl.ds(to, TPF), :] = sum_ref[pl.ds(fr, TPF), :]
        return carry

    lax.fori_loop(0, FPD, place, 0)


def dispatch(owners, own, others):
    vm = pl.BlockSpec(memory_space=pltpu.VMEM)
    return pl.pallas_call(
        dispatch_kernel,
        out_shape=jax.ShapeDtypeStruct((SLOT_ROWS, 2 * HD), jnp.bfloat16),
        in_specs=[pl.BlockSpec(memory_space=pltpu.SMEM)] + [vm] * 4,
        out_specs=vm,
        scratch_shapes=[pltpu.VMEM((BLOCK, 2 * HD), jnp.bfloat16), pltpu.SMEM((N_VID,), jnp.int32)],
        compiler_params=pltpu.CompilerParams(vmem_limit_bytes=SMALL),
        cost_estimate=pl.CostEstimate(flops=0, bytes_accessed=2 << 20, transcendentals=0),
        name="dispatch",
    )(owners, own, *others)


PIECES = [(dx, other) for dx in (0, -1, 1, 2) for other in (False, True)]


def merge_kernel(_, wk_ref, wv_ref, out_ref):
    x, core = lax.axis_index("x"), lax.axis_index("core")
    for p, (dx, other) in enumerate(PIECES):
        by = 1 - core if other else core
        h = ((x + dx * (1 - 2 * by) + NX) % NX) * 2 + by
        at = pl.ds(pl.multiple_of(h * HD, HD), HD)
        out_ref[:, 2 * p * HD : (2 * p + 1) * HD] = wk_ref[:, at]
        out_ref[:, (2 * p + 1) * HD : (2 * p + 2) * HD] = wv_ref[:, at]


def merge(after, key_weight, value_weight):
    vm = pl.BlockSpec(memory_space=pltpu.VMEM)
    return pl.pallas_call(
        merge_kernel,
        out_shape=jax.ShapeDtypeStruct((key_weight.shape[0], 2 * KVH * HD), jnp.bfloat16),
        in_specs=[pl.BlockSpec(memory_space=pl.ANY), vm, vm],
        out_specs=vm,
        compiler_params=pltpu.CompilerParams(vmem_limit_bytes=SMALL),
        cost_estimate=pl.CostEstimate(flops=0, bytes_accessed=8 << 20, transcendentals=0),
        name="merge",
    )(after, key_weight, value_weight)


def project(name, pieces, first, weight, total=None):
    cols = weight.shape[0]
    n = len(pieces)
    tile = 512
    n_tile = SLOT_ROWS // tile
    final = total is not None
    feats = slice(2 * HD * first, 2 * HD * (first + n))

    def product(refs, w_ref, rows):
        a = jnp.concatenate([ref[rows, :] for ref in refs[:n]], axis=1)
        return dot32(a, w_ref[:, feats], NT)

    def body_first(*refs):
        w_ref, out_ref = refs[n:]
        for t in range(n_tile):
            rows = slice(t * tile, (t + 1) * tile)
            out_ref[rows, :] = product(refs, w_ref, rows)

    def body_final(*refs):
        w_ref, total_ref, out_ref, out_at, sems = refs[n:]
        copies = []
        for t in range(n_tile):
            rows = slice(t * tile, (t + 1) * tile)
            out_at[rows, :] = (total_ref[rows, :] + product(refs, w_ref, rows)).astype(jnp.bfloat16)
            copy = pltpu.make_async_copy(out_at.at[rows, :], out_ref.at[rows, :], sems.at[t])
            copy.start()
            copies.append(copy)
        for copy in copies:
            copy.wait()

    vm = pl.BlockSpec(memory_space=pltpu.VMEM)
    scratch = [pltpu.VMEM((SLOT_ROWS, cols), jnp.bfloat16), pltpu.SemaphoreType.DMA((n_tile,))]
    return pl.pallas_call(
        body_final if final else body_first,
        out_shape=jax.ShapeDtypeStruct((SLOT_ROWS, cols), jnp.bfloat16 if final else jnp.float32),
        in_specs=[vm] * (n + 1 + final),
        out_specs=pl.BlockSpec(memory_space=pltpu.HBM) if final else vm,
        scratch_shapes=scratch if final else [],
        compiler_params=pltpu.CompilerParams(vmem_limit_bytes=MIDDLE),
        cost_estimate=pl.CostEstimate(
            flops=4 * SLOT_ROWS * cols * n * HD, bytes_accessed=6 << 20, transcendentals=0
        ),
        name=name,
    )(*pieces, weight, *([total] if final else []))


def finish_kernel(keep_ref, a_ref, b_ref, c_ref, out_ref):
    total = keep_ref[...]
    for ref in (a_ref, b_ref, c_ref):
        total = total + ref[...].astype(jnp.float32)
    total = (total * SCALE).T
    for h in range(GROUP):
        out_ref[:, h * HD : (h + 1) * HD] = total[h * QLEN : (h + 1) * QLEN, :].astype(jnp.bfloat16)


def finish(keep, others):
    return pl.pallas_call(
        finish_kernel,
        out_shape=jax.ShapeDtypeStruct((QLEN, GROUP * HD), jnp.bfloat16),
        compiler_params=pltpu.CompilerParams(vmem_limit_bytes=SMALL),
        cost_estimate=pl.CostEstimate(flops=0, bytes_accessed=1 << 19, transcendentals=0),
        name="finish",
    )(keep, *others)


def on_device(
    queries,
    out_grad,
    log_totals,
    out_dots,
    lengths,
    vis_keys,
    vis_values,
    key_weight,
    value_weight,
    frame_owner,
):
    msg, kv0 = pack(
        lengths, queries, out_grad, log_totals, out_dots, vis_keys, vis_values
    )

    kv_up, kv_down = shift(kv0, "y", 1), shift(kv0, "y", -1)
    up1, down1 = shift(msg, "z", 1), shift(msg, "z", -1)
    away = [kv_up, kv_down, shift(kv0, "y", 2)]
    up2, down2 = shift(up1, "z", 1), shift(down1, "z", -1)
    bf16, f32 = jnp.bfloat16, jnp.float32
    none = [None] * NY

    near = [msg, up1, down1]
    dq, (own,) = attend("home_first", near, [kv0], none[:1], none[:3], [f32] * 3, f32, False)
    up2, down2, own = lax.optimization_barrier((up2, down2, own))
    up3, down3 = shift(up2, "z", 1), shift(down2, "z", -1)
    dq, acc = attend("away_near", near, away, none[:3], dq, [f32, bf16, bf16], f32, False)
    dq_0, dq_u1, dq_d1 = dq
    up3, down3, dq_0 = lax.optimization_barrier((up3, down3, dq_0))
    far = shift(up3, "z", 1)
    two = [up2, down2]
    (dq_u2, dq_d2), acc = attend("away_two", two, away, acc, none[:2], [f32] * 2, f32, False)
    three = [up3, down3]
    (odd,), acc = attend(
        "all_three", three, away + [kv0], acc + [own], none[:2], bf16, f32, False, (dq_u1, dq_d1)
    )
    own = acc.pop()
    (dq_4,), parts = attend("away_far", [far], away, acc, none[:1], [f32], bf16, True)

    part_up, part_down, part_far = parts
    back = (shift(part_far, "y", 2), shift(part_up, "y", -1), shift(part_down, "y", 1))
    got = lax.ppermute(odd, "zp", [(0, 1), (1, 0)])
    dq, (own,) = attend(
        "home_last", two + [far], [kv0], [own], [dq_u2, dq_d2, dq_4], [f32] * 3, f32, True
    )
    even = [dq_0, dq[1], dq[0], dq[2]]

    keep, *sends = pair(even, got)
    own, keep = lax.optimization_barrier((own, keep))

    outgoing = dispatch(frame_owner.reshape(-1), own, back)
    mine = lax.all_to_all(outgoing, Z + ("y",), split_axis=0, concat_axis=0, tiled=True)
    mine, *sends = lax.optimization_barrier((mine, *sends))

    first, second = shift_by_core(mine, 1), shift_by_core(mine, -1)
    others = [shift(rows, "z", offset) for rows, offset in zip(sends, EVEN[1:])]
    pieces = [mine, shift(mine, "core", 1)]
    first, second, *others = lax.optimization_barrier((first, second, *others))
    across = shift_by_core(first, 1)
    for rows in (first, second):
        pieces += [rows, shift(rows, "core", 1)]
    query_grad = finish(keep, others)
    weight = merge(first, key_weight, value_weight)
    total = project("project_near", pieces, 0, weight)
    across, total, query_grad = lax.optimization_barrier((across, total, query_grad))
    pieces = [across, shift(across, "core", 1)]
    return query_grad, project("project_across", pieces, 6, weight, total)


def solution(mesh):
    devices = mesh.devices.reshape(NZ // 2, 2, NY, NX, 2)
    split = jax.sharding.Mesh(devices, Z + ("y", "x", "core"))
    vid, head = Z + ("y",), ("x", "core")
    in_specs = (
        P(vid, head),
        P(vid, head),
        P(head, vid),
        P(head, vid),
        P(),
        P(vid, head),
        P(vid, head),
        P(head, None),
        P(head, None),
        P(),
    )
    out_specs = (P(vid, head), P(vid, head))
    return jax.shard_map(
        on_device, mesh=split, in_specs=in_specs, out_specs=out_specs, check_vma=False
    )
```

```python
import math

import jax
import jax.numpy as jnp
from jax import lax
from jax.experimental import pallas as pl
from jax.experimental.pallas import tpu as pltpu
from jax.sharding import PartitionSpec as P

QH = 64
KVH = 8
HD = 128
TPF = 16
QLEN = 64
GROUP = QH // KVH
ROWS = GROUP * QLEN
NZ = 8
NY = 4
NX = 4
Z = ("zq", "zp")
BLOCK = 512
MSG = 2 * QLEN + 16
FPD = 32
MOST = 2
N_VID = NZ * NY
SLOT_ROWS = N_VID * MOST * TPF
SCALE = HD ** (-0.5)
LOG2E = math.log2(math.e)
DEAD = 1e30
ORDER = (0, -1, 1, -2, 2, -3, 3, 4)
EVEN = (0, 2, -2, 4)
ODD = (-1, 1, -3, 3)
VMEM = 20 * 1024 * 1024
SMALL = 8 * 1024 * 1024
MIDDLE = 12 * 1024 * 1024


SIZES = {"z": NZ, "y": NY, "x": NX, "core": 2}


def shift(a, axis, k):
    n = SIZES[axis]
    return lax.ppermute(a, Z if axis == "z" else axis, [(i, (i + k) % n) for i in range(n)])


def shift_by_core(a, k):
    pairs = []
    for x in range(NX):
        for core, by in ((0, k), (1, -k)):
            pairs.append((2 * x + core, 2 * ((x + by) % NX) + core))
    return lax.ppermute(a, ("x", "core"), pairs)


def vid_index():
    return (lax.axis_index("zq") * 2 + lax.axis_index("zp")) * NY + lax.axis_index("y")


def run_copies(pairs, sems):
    copies = [pltpu.make_async_copy(src, dst, sems.at[i]) for i, (src, dst) in enumerate(pairs)]
    for copy in copies:
        copy.start()
    return copies


def pack_kernel(
    len_ref, q_ref, g_ref, total_ref, dot_ref, k_ref, v_ref, msg_ref, kv_ref,
    len_at, total_at, dot_at, sems,
):
    f32 = jnp.float32
    copies = run_copies(
        [
            (len_ref, len_at),
            (total_ref, total_at),
            (dot_ref, dot_at),
            (q_ref, msg_ref.at[0:QLEN, :]),
            (g_ref, msg_ref.at[QLEN : 2 * QLEN, :]),
            (k_ref, kv_ref.at[:, 0:HD]),
            (v_ref, kv_ref.at[:, HD : 2 * HD]),
        ],
        sems,
    )
    for copy in copies[:3]:
        copy.wait()
    row = lax.broadcasted_iota(jnp.int32, (GROUP, QLEN), 1)
    total = jnp.where(row < len_at[vid_index()], total_at[...].astype(f32), DEAD)
    dots = dot_at[...].astype(f32)
    line = [total[h : h + 1, :] for h in range(GROUP)] + [dots[h : h + 1, :] for h in range(GROUP)]
    line = jnp.concatenate(line, axis=1)
    msg_ref[2 * QLEN :, :] = jnp.broadcast_to(line, (MSG - 2 * QLEN, 2 * ROWS)).astype(jnp.bfloat16)
    for copy in copies[3:]:
        copy.wait()


def pack(lengths, queries, out_grad, log_totals, out_dots, vis_keys, vis_values):
    vm = pl.BlockSpec(memory_space=pltpu.VMEM)
    hbm = pl.BlockSpec(memory_space=pltpu.HBM)
    return pl.pallas_call(
        pack_kernel,
        out_shape=[
            jax.ShapeDtypeStruct((MSG, GROUP * HD), jnp.bfloat16),
            jax.ShapeDtypeStruct((BLOCK, 2 * HD), jnp.bfloat16),
        ],
        in_specs=[hbm] * 7,
        out_specs=[vm, vm],
        scratch_shapes=[
            pltpu.SMEM(lengths.shape, jnp.int32),
            pltpu.VMEM((GROUP, QLEN), jnp.bfloat16),
            pltpu.VMEM((GROUP, QLEN), jnp.bfloat16),
            pltpu.SemaphoreType.DMA((7,)),
        ],
        cost_estimate=pl.CostEstimate(flops=0, bytes_accessed=1 << 20, transcendentals=0),
        name="pack",
    )(lengths, queries, out_grad, log_totals, out_dots, vis_keys, vis_values)


def heads_as_rows(block):
    return jnp.concatenate([block[:, h * HD : (h + 1) * HD] for h in range(GROUP)], axis=0)


NT = (((1,), (1,)), ((), ()))
NN = (((1,), (0,)), ((), ()))
TN = (((0,), (0,)), ((), ()))


def dot32(a, b, contract):
    return lax.dot_general(a, b, contract, preferred_element_type=jnp.float32)


def load_message(ref, c, q_at, g_at, stat_at):
    rows = slice(c * ROWS, (c + 1) * ROWS)
    q_at[rows, :] = heads_as_rows(ref[0:QLEN, :])
    g_at[rows, :] = heads_as_rows(ref[QLEN : 2 * QLEN, :])
    stats = ref[2 * QLEN : MSG, :].astype(jnp.float32)[0:8, :]
    stat_at[8 * c : 8 * c + 8, 0:ROWS] = stats[:, :ROWS] * LOG2E
    stat_at[8 * c : 8 * c + 8, ROWS:] = stats[:, ROWS:]


def attend_tile(c, kv_ref, q_at, g_at, stat_at):
    rows = pl.ds(pl.multiple_of(c * ROWS, ROWS), ROWS)
    q, g = q_at[rows, :], g_at[rows, :]
    stat = pl.ds(pl.multiple_of(c * 8, 8), 8)
    total, dots = stat_at[stat, 0:ROWS][0:1, :], stat_at[stat, ROWS:][0:1, :]
    k, v = kv_ref[:, 0:HD], kv_ref[:, HD : 2 * HD]
    p = jnp.exp2(dot32(k, q, NT) * (SCALE * LOG2E) - total)
    ds = (p * (dot32(v, g, NT) - dots)).astype(jnp.bfloat16)
    dv = dot32(p.astype(jnp.bfloat16), g, NN)
    return dot32(ds, q, NN), dv, dot32(k, ds, TN)


def message_scratch(n):
    return [
        pltpu.VMEM((n * ROWS, HD), jnp.bfloat16),
        pltpu.VMEM((n * ROWS, HD), jnp.bfloat16),
        pltpu.VMEM((8 * n, 2 * ROWS), jnp.float32),
    ]


def attend(name, messages, blocks, accs, dqs, dq_type, acc_type, final, odd=None):
    n, nb = len(messages), len(blocks)
    in_acc = [a for a in accs if a is not None]
    in_dq = [a for a in dqs if a is not None]
    in_odd = list(odd) if odd else []
    operands = list(messages) + list(blocks) + in_acc + in_dq + in_odd
    n_in = len(operands)
    n_dq = 1 if odd else n
    in_place = acc_type == jnp.float32 and len(in_acc) == nb
    aliases = {n + nb + b: n_dq + b for b in range(nb)} if in_place else {}

    def body(*refs):
        ins = list(refs[:n_in])
        dq_refs = refs[n_in : n_in + n_dq]
        out_refs = refs[n_in + n_dq : n_in + n_dq + nb]
        q_at, g_at, stat_at, dq_at = refs[n_in + n_dq + nb :]
        take = lambda count: [ins.pop(0) for _ in range(count)]
        msg_refs, kv_refs = take(n), take(nb)
        acc_refs = [take(1)[0] if a is not None else None for a in accs]
        dq_ins = [take(1)[0] if a is not None else None for a in dqs]
        for c in range(n):
            load_message(msg_refs[c], c, q_at, g_at, stat_at)
            if dq_ins[c] is not None:
                dq_at[c * HD : (c + 1) * HD, :] = dq_ins[c][...]
        if not in_place and n > 1:
            for b in range(nb):
                out_refs[b][...] = jnp.zeros_like(out_refs[b])

        def step(c, carry):
            dq = 0.0
            for b in range(nb):
                dk, dv, dq_b = attend_tile(c, kv_refs[b], q_at, g_at, stat_at)
                dq = dq + dq_b
                if n == 1:
                    if acc_refs[b] is not None:
                        dk = dk + acc_refs[b][:, 0:HD]
                        dv = dv + acc_refs[b][:, HD : 2 * HD]
                    if final:
                        dk = dk * SCALE
                    out_refs[b][:, 0:HD] = dk.astype(acc_type)
                    out_refs[b][:, HD : 2 * HD] = dv.astype(acc_type)
                else:
                    out_refs[b][:, 0:HD] += dk
                    out_refs[b][:, HD : 2 * HD] += dv
            rows = pl.ds(pl.multiple_of(c * HD, HD), HD)
            dq_at[rows, :] = dq_at[rows, :] + dq if in_dq else dq
            return carry

        if n == 1 or nb == 1:
            for c in range(n):
                step(c, 0)
        else:
            lax.fori_loop(0, n, step, 0)
        if final and n > 1:
            for b in range(nb):
                out_refs[b][:, 0:HD] = out_refs[b][:, 0:HD] * SCALE
        if odd:
            for c, ref in enumerate(ins):
                dq_refs[0][c * HD : (c + 1) * HD, :] = ref[...]
            dq_refs[0][len(ins) * HD :, :] = dq_at[...].astype(dq_type)
        else:
            for c in range(n):
                dq_refs[c][...] = dq_at[c * HD : (c + 1) * HD, :].astype(dq_type[c])

    if odd:
        out_shape = [jax.ShapeDtypeStruct(((len(in_odd) + n) * HD, ROWS), dq_type)]
    else:
        out_shape = [jax.ShapeDtypeStruct((HD, ROWS), t) for t in dq_type]
    out_shape += [jax.ShapeDtypeStruct((BLOCK, 2 * HD), acc_type)] * nb
    outs = pl.pallas_call(
        body,
        out_shape=out_shape,
        scratch_shapes=message_scratch(n) + [pltpu.VMEM((n * HD, ROWS), jnp.float32)],
        input_output_aliases=aliases,
        compiler_params=pltpu.CompilerParams(vmem_limit_bytes=VMEM),
        cost_estimate=pl.CostEstimate(
            flops=n * 20 * ROWS * nb * BLOCK * HD,
            bytes_accessed=2 << 20,
            transcendentals=n * ROWS * nb * BLOCK,
        ),
        name=name,
    )(*operands)
    return list(outs[:n_dq]), list(outs[n_dq:])


def pair_kernel(got_ref, *refs):
    even_refs, keep_ref, send_refs = refs[: len(EVEN)], refs[len(EVEN)], refs[len(EVEN) + 1 :]
    away = 1 - 2 * (lax.axis_index("zp"))
    for i, offset in enumerate(EVEN):
        there = (offset - away + NZ) % NZ
        slot = jnp.int32(0)
        for j, odd in enumerate(ODD):
            slot = jnp.where(there == odd % NZ, j, slot)
        got = got_ref[pl.ds(pl.multiple_of(slot * HD, HD), HD), :].astype(jnp.float32)
        total = even_refs[i][...] + got
        if i == 0:
            keep_ref[...] = total
        else:
            send_refs[i - 1][...] = total.astype(jnp.bfloat16)


def pair(even, got):
    vm = pl.BlockSpec(memory_space=pltpu.VMEM)
    return pl.pallas_call(
        pair_kernel,
        out_shape=[jax.ShapeDtypeStruct((HD, ROWS), jnp.float32)]
        + [jax.ShapeDtypeStruct((HD, ROWS), jnp.bfloat16)] * 3,
        in_specs=[vm] * 5,
        out_specs=[vm] * 4,
        compiler_params=pltpu.CompilerParams(vmem_limit_bytes=SMALL),
        cost_estimate=pl.CostEstimate(flops=0, bytes_accessed=2 << 20, transcendentals=0),
        name="pair",
    )(got, *even)


def dispatch_kernel(owner_ref, own_ref, a_ref, b_ref, c_ref, out_ref, sum_ref, count_ref):
    f32 = jnp.float32
    total = own_ref[...] + a_ref[...].astype(f32) + b_ref[...].astype(f32) + c_ref[...].astype(f32)
    sum_ref[...] = total.astype(jnp.bfloat16)
    out_ref[...] = jnp.zeros_like(out_ref)
    for j in range(N_VID):
        count_ref[j] = 0

    first = vid_index() * FPD

    def place(f, carry):
        owner = owner_ref[first + f]
        slot = count_ref[owner]
        count_ref[owner] = slot + 1
        to = pl.multiple_of((owner * MOST + slot) * TPF, TPF)
        fr = pl.multiple_of(f * TPF, TPF)
        out_ref[pl.ds(to, TPF), :] = sum_ref[pl.ds(fr, TPF), :]
        return carry

    lax.fori_loop(0, FPD, place, 0)


def dispatch(owners, own, others):
    vm = pl.BlockSpec(memory_space=pltpu.VMEM)
    return pl.pallas_call(
        dispatch_kernel,
        out_shape=jax.ShapeDtypeStruct((SLOT_ROWS, 2 * HD), jnp.bfloat16),
        in_specs=[pl.BlockSpec(memory_space=pltpu.SMEM)] + [vm] * 4,
        out_specs=vm,
        scratch_shapes=[pltpu.VMEM((BLOCK, 2 * HD), jnp.bfloat16), pltpu.SMEM((N_VID,), jnp.int32)],
        compiler_params=pltpu.CompilerParams(vmem_limit_bytes=SMALL),
        cost_estimate=pl.CostEstimate(flops=0, bytes_accessed=2 << 20, transcendentals=0),
        name="dispatch",
    )(owners, own, *others)


PIECES = [(dx, other) for dx in (0, -1, 1, 2) for other in (False, True)]


def merge_kernel(_, wk_ref, wv_ref, out_ref):
    x, core = lax.axis_index("x"), lax.axis_index("core")
    for p, (dx, other) in enumerate(PIECES):
        by = 1 - core if other else core
        h = ((x + dx * (1 - 2 * by) + NX) % NX) * 2 + by
        at = pl.ds(pl.multiple_of(h * HD, HD), HD)
        out_ref[:, 2 * p * HD : (2 * p + 1) * HD] = wk_ref[:, at]
        out_ref[:, (2 * p + 1) * HD : (2 * p + 2) * HD] = wv_ref[:, at]


def merge(after, key_weight, value_weight):
    vm = pl.BlockSpec(memory_space=pltpu.VMEM)
    return pl.pallas_call(
        merge_kernel,
        out_shape=jax.ShapeDtypeStruct((key_weight.shape[0], 2 * KVH * HD), jnp.bfloat16),
        in_specs=[pl.BlockSpec(memory_space=pl.ANY), vm, vm],
        out_specs=vm,
        compiler_params=pltpu.CompilerParams(vmem_limit_bytes=SMALL),
        cost_estimate=pl.CostEstimate(flops=0, bytes_accessed=8 << 20, transcendentals=0),
        name="merge",
    )(after, key_weight, value_weight)


def project(name, pieces, first, weight, total=None):
    cols = weight.shape[0]
    n = len(pieces)
    final = total is not None
    tile = 256 if final else 512
    n_tile = SLOT_ROWS // tile
    feats = slice(2 * HD * first, 2 * HD * (first + n))

    def product(refs, w_ref, rows):
        a = jnp.concatenate([ref[rows, :] for ref in refs[:n]], axis=1)
        return dot32(a, w_ref[:, feats], NT)

    def body_first(*refs):
        w_ref, out_ref = refs[n:]
        for t in range(n_tile):
            rows = slice(t * tile, (t + 1) * tile)
            out_ref[rows, :] = product(refs, w_ref, rows)

    def body_final(*refs):
        w_ref, total_ref, out_ref, out_at, sems = refs[n:]
        copies = []
        for t in range(n_tile):
            rows = slice(t * tile, (t + 1) * tile)
            out_at[rows, :] = (total_ref[rows, :] + product(refs, w_ref, rows)).astype(jnp.bfloat16)
            copy = pltpu.make_async_copy(out_at.at[rows, :], out_ref.at[rows, :], sems.at[t])
            copy.start()
            copies.append(copy)
        for copy in copies:
            copy.wait()

    vm = pl.BlockSpec(memory_space=pltpu.VMEM)
    scratch = [pltpu.VMEM((SLOT_ROWS, cols), jnp.bfloat16), pltpu.SemaphoreType.DMA((n_tile,))]
    return pl.pallas_call(
        body_final if final else body_first,
        out_shape=jax.ShapeDtypeStruct((SLOT_ROWS, cols), jnp.bfloat16 if final else jnp.float32),
        in_specs=[vm] * (n + 1 + final),
        out_specs=pl.BlockSpec(memory_space=pltpu.HBM) if final else vm,
        scratch_shapes=scratch if final else [],
        compiler_params=pltpu.CompilerParams(vmem_limit_bytes=MIDDLE),
        cost_estimate=pl.CostEstimate(
            flops=4 * SLOT_ROWS * cols * n * HD, bytes_accessed=6 << 20, transcendentals=0
        ),
        name=name,
    )(*pieces, weight, *([total] if final else []))


def finish_kernel(keep_ref, a_ref, b_ref, c_ref, out_ref):
    total = keep_ref[...]
    for ref in (a_ref, b_ref, c_ref):
        total = total + ref[...].astype(jnp.float32)
    total = (total * SCALE).T
    for h in range(GROUP):
        out_ref[:, h * HD : (h + 1) * HD] = total[h * QLEN : (h + 1) * QLEN, :].astype(jnp.bfloat16)


def finish(keep, others):
    return pl.pallas_call(
        finish_kernel,
        out_shape=jax.ShapeDtypeStruct((QLEN, GROUP * HD), jnp.bfloat16),
        compiler_params=pltpu.CompilerParams(vmem_limit_bytes=SMALL),
        cost_estimate=pl.CostEstimate(flops=0, bytes_accessed=1 << 19, transcendentals=0),
        name="finish",
    )(keep, *others)


def on_device(
    queries,
    out_grad,
    log_totals,
    out_dots,
    lengths,
    vis_keys,
    vis_values,
    key_weight,
    value_weight,
    frame_owner,
):
    msg, kv0 = pack(
        lengths, queries, out_grad, log_totals, out_dots, vis_keys, vis_values
    )

    kv_up, kv_down = shift(kv0, "y", 1), shift(kv0, "y", -1)
    up1, down1 = shift(msg, "z", 1), shift(msg, "z", -1)
    away = [kv_up, kv_down, shift(kv0, "y", 2)]
    up2, down2 = shift(up1, "z", 1), shift(down1, "z", -1)
    bf16, f32 = jnp.bfloat16, jnp.float32
    none = [None] * NY

    near = [msg, up1, down1]
    dq, (own,) = attend("home_first", near, [kv0], none[:1], none[:3], [f32] * 3, f32, False)
    up2, down2, own = lax.optimization_barrier((up2, down2, own))
    up3, down3 = shift(up2, "z", 1), shift(down2, "z", -1)
    dq, acc = attend("away_near", near, away, none[:3], dq, [f32, bf16, bf16], f32, False)
    dq_0, dq_u1, dq_d1 = dq
    up3, down3, dq_0 = lax.optimization_barrier((up3, down3, dq_0))
    far = shift(up3, "z", 1)
    two = [up2, down2]
    (dq_u2, dq_d2), acc = attend("away_two", two, away, acc, none[:2], [f32] * 2, f32, False)
    three = [up3, down3]
    (odd,), acc = attend(
        "all_three", three, away + [kv0], acc + [own], none[:2], bf16, f32, False, (dq_u1, dq_d1)
    )
    own = acc.pop()
    (dq_4,), parts = attend("away_far", [far], away, acc, none[:1], [f32], bf16, True)

    part_up, part_down, part_far = parts
    back = (shift(part_far, "y", 2), shift(part_up, "y", -1), shift(part_down, "y", 1))
    got = lax.ppermute(odd, "zp", [(0, 1), (1, 0)])
    dq, (own,) = attend(
        "home_last", two + [far], [kv0], [own], [dq_u2, dq_d2, dq_4], [f32] * 3, f32, True
    )
    even = [dq_0, dq[1], dq[0], dq[2]]

    keep, *sends = pair(even, got)
    own, keep = lax.optimization_barrier((own, keep))

    outgoing = dispatch(frame_owner.reshape(-1), own, back)
    mine = lax.all_to_all(outgoing, Z + ("y",), split_axis=0, concat_axis=0, tiled=True)
    mine, *sends = lax.optimization_barrier((mine, *sends))

    first, second = shift_by_core(mine, 1), shift_by_core(mine, -1)
    others = [shift(rows, "z", offset) for rows, offset in zip(sends, EVEN[1:])]
    pieces = [mine, shift(mine, "core", 1)]
    first, second, others[0], others[1] = lax.optimization_barrier(
        (first, second, others[0], others[1])
    )
    across = shift_by_core(first, 1)
    for rows in (first, second):
        pieces += [rows, shift(rows, "core", 1)]
    weight = merge(first, key_weight, value_weight)
    total = project("project_near", pieces, 0, weight)
    others[2], total = lax.optimization_barrier((others[2], total))
    across, total = lax.optimization_barrier((across, total))
    pieces = [across, shift(across, "core", 1)]
    query_grad = finish(keep, others)
    total, query_grad = lax.optimization_barrier((total, query_grad))
    return query_grad, project("project_across", pieces, 6, weight, total)


def solution(mesh):
    devices = mesh.devices.reshape(NZ // 2, 2, NY, NX, 2)
    split = jax.sharding.Mesh(devices, Z + ("y", "x", "core"))
    vid, head = Z + ("y",), ("x", "core")
    in_specs = (
        P(vid, head),
        P(vid, head),
        P(head, vid),
        P(head, vid),
        P(),
        P(vid, head),
        P(vid, head),
        P(head, None),
        P(head, None),
        P(),
    )
    out_specs = (P(vid, head), P(vid, head))
    return jax.shard_map(
        on_device, mesh=split, in_specs=in_specs, out_specs=out_specs, check_vma=False
    )
```

```python
import math

import jax
import jax.numpy as jnp
from jax import lax
from jax.experimental import pallas as pl
from jax.experimental.pallas import tpu as pltpu
from jax.sharding import PartitionSpec as P

QH = 64
KVH = 8
HD = 128
TPF = 16
QLEN = 64
GROUP = QH // KVH
ROWS = GROUP * QLEN
NZ = 8
NY = 4
NX = 4
Z = ("zq", "zp")
BLOCK = 512
MSG = 2 * QLEN + 16
FPD = 32
MOST = 2
N_VID = NZ * NY
SLOT_ROWS = N_VID * MOST * TPF
SCALE = HD ** (-0.5)
LOG2E = math.log2(math.e)
DEAD = 1e30
ORDER = (0, -1, 1, -2, 2, -3, 3, 4)
EVEN = (0, 2, -2, 4)
ODD = (-1, 1, -3, 3)
VMEM = 20 * 1024 * 1024
SMALL = 8 * 1024 * 1024
MIDDLE = 12 * 1024 * 1024


SIZES = {"z": NZ, "y": NY, "x": NX, "core": 2}


def shift(a, axis, k):
    n = SIZES[axis]
    return lax.ppermute(a, Z if axis == "z" else axis, [(i, (i + k) % n) for i in range(n)])


def shift_by_core(a, k):
    pairs = []
    for x in range(NX):
        for core, by in ((0, k), (1, -k)):
            pairs.append((2 * x + core, 2 * ((x + by) % NX) + core))
    return lax.ppermute(a, ("x", "core"), pairs)


def vid_index():
    return (lax.axis_index("zq") * 2 + lax.axis_index("zp")) * NY + lax.axis_index("y")


def run_copies(pairs, sems):
    copies = [pltpu.make_async_copy(src, dst, sems.at[i]) for i, (src, dst) in enumerate(pairs)]
    for copy in copies:
        copy.start()
    return copies


def pack_kernel(
    len_ref, q_ref, g_ref, total_ref, dot_ref, k_ref, v_ref, msg_ref, kv_ref,
    len_at, total_at, dot_at, sems,
):
    f32 = jnp.float32
    copies = run_copies(
        [
            (len_ref, len_at),
            (total_ref, total_at),
            (dot_ref, dot_at),
            (q_ref, msg_ref.at[0:QLEN, :]),
            (g_ref, msg_ref.at[QLEN : 2 * QLEN, :]),
            (k_ref, kv_ref.at[:, 0:HD]),
            (v_ref, kv_ref.at[:, HD : 2 * HD]),
        ],
        sems,
    )
    for copy in copies[:3]:
        copy.wait()
    row = lax.broadcasted_iota(jnp.int32, (GROUP, QLEN), 1)
    total = jnp.where(row < len_at[vid_index()], total_at[...].astype(f32), DEAD)
    dots = dot_at[...].astype(f32)
    line = [total[h : h + 1, :] for h in range(GROUP)] + [dots[h : h + 1, :] for h in range(GROUP)]
    line = jnp.concatenate(line, axis=1)
    msg_ref[2 * QLEN :, :] = jnp.broadcast_to(line, (MSG - 2 * QLEN, 2 * ROWS)).astype(jnp.bfloat16)
    for copy in copies[3:]:
        copy.wait()


def pack(lengths, queries, out_grad, log_totals, out_dots, vis_keys, vis_values):
    vm = pl.BlockSpec(memory_space=pltpu.VMEM)
    hbm = pl.BlockSpec(memory_space=pltpu.HBM)
    return pl.pallas_call(
        pack_kernel,
        out_shape=[
            jax.ShapeDtypeStruct((MSG, GROUP * HD), jnp.bfloat16),
            jax.ShapeDtypeStruct((BLOCK, 2 * HD), jnp.bfloat16),
        ],
        in_specs=[hbm] * 7,
        out_specs=[vm, vm],
        scratch_shapes=[
            pltpu.SMEM(lengths.shape, jnp.int32),
            pltpu.VMEM((GROUP, QLEN), jnp.bfloat16),
            pltpu.VMEM((GROUP, QLEN), jnp.bfloat16),
            pltpu.SemaphoreType.DMA((7,)),
        ],
        cost_estimate=pl.CostEstimate(flops=0, bytes_accessed=1 << 20, transcendentals=0),
        name="pack",
    )(lengths, queries, out_grad, log_totals, out_dots, vis_keys, vis_values)


def heads_as_rows(block):
    return jnp.concatenate([block[:, h * HD : (h + 1) * HD] for h in range(GROUP)], axis=0)


NT = (((1,), (1,)), ((), ()))
NN = (((1,), (0,)), ((), ()))
TN = (((0,), (0,)), ((), ()))


def dot32(a, b, contract):
    return lax.dot_general(a, b, contract, preferred_element_type=jnp.float32)


def load_message(ref, c, q_at, g_at, stat_at):
    rows = slice(c * ROWS, (c + 1) * ROWS)
    q_at[rows, :] = heads_as_rows(ref[0:QLEN, :])
    g_at[rows, :] = heads_as_rows(ref[QLEN : 2 * QLEN, :])
    stats = ref[2 * QLEN : MSG, :].astype(jnp.float32)[0:8, :]
    stat_at[8 * c : 8 * c + 8, 0:ROWS] = stats[:, :ROWS] * LOG2E
    stat_at[8 * c : 8 * c + 8, ROWS:] = stats[:, ROWS:]


def attend_tile(c, kv_ref, q_at, g_at, stat_at):
    rows = pl.ds(pl.multiple_of(c * ROWS, ROWS), ROWS)
    q, g = q_at[rows, :], g_at[rows, :]
    stat = pl.ds(pl.multiple_of(c * 8, 8), 8)
    total, dots = stat_at[stat, 0:ROWS][0:1, :], stat_at[stat, ROWS:][0:1, :]
    k, v = kv_ref[:, 0:HD], kv_ref[:, HD : 2 * HD]
    p = jnp.exp2(dot32(k, q, NT) * (SCALE * LOG2E) - total)
    ds = (p * (dot32(v, g, NT) - dots)).astype(jnp.bfloat16)
    dv = dot32(p.astype(jnp.bfloat16), g, NN)
    return dot32(ds, q, NN), dv, dot32(k, ds, TN)


def message_scratch(n):
    return [
        pltpu.VMEM((n * ROWS, HD), jnp.bfloat16),
        pltpu.VMEM((n * ROWS, HD), jnp.bfloat16),
        pltpu.VMEM((8 * n, 2 * ROWS), jnp.float32),
    ]


def attend(name, messages, blocks, accs, dqs, dq_type, acc_type, final, odd=None):
    n, nb = len(messages), len(blocks)
    in_acc = [a for a in accs if a is not None]
    in_dq = [a for a in dqs if a is not None]
    in_odd = list(odd) if odd else []
    operands = list(messages) + list(blocks) + in_acc + in_dq + in_odd
    n_in = len(operands)
    n_dq = 1 if odd else n
    in_place = acc_type == jnp.float32
    given = [b for b in range(nb) if accs[b] is not None]
    aliases = {n + nb + i: n_dq + b for i, b in enumerate(given)} if in_place else {}

    def body(*refs):
        ins = list(refs[:n_in])
        dq_refs = refs[n_in : n_in + n_dq]
        out_refs = refs[n_in + n_dq : n_in + n_dq + nb]
        q_at, g_at, stat_at, dq_at = refs[n_in + n_dq + nb :]
        take = lambda count: [ins.pop(0) for _ in range(count)]
        msg_refs, kv_refs = take(n), take(nb)
        acc_refs = [take(1)[0] if a is not None else None for a in accs]
        dq_ins = [take(1)[0] if a is not None else None for a in dqs]
        for c in range(n):
            load_message(msg_refs[c], c, q_at, g_at, stat_at)
            if dq_ins[c] is not None:
                dq_at[c * HD : (c + 1) * HD, :] = dq_ins[c][...]
        if n > 1:
            for b in range(nb):
                if acc_refs[b] is None:
                    out_refs[b][...] = jnp.zeros_like(out_refs[b])

        def step(c, carry):
            dq = 0.0
            for b in range(nb):
                dk, dv, dq_b = attend_tile(c, kv_refs[b], q_at, g_at, stat_at)
                dq = dq + dq_b
                if n == 1:
                    if acc_refs[b] is not None:
                        dk = dk + acc_refs[b][:, 0:HD]
                        dv = dv + acc_refs[b][:, HD : 2 * HD]
                    if final:
                        dk = dk * SCALE
                    out_refs[b][:, 0:HD] = dk.astype(acc_type)
                    out_refs[b][:, HD : 2 * HD] = dv.astype(acc_type)
                else:
                    out_refs[b][:, 0:HD] += dk
                    out_refs[b][:, HD : 2 * HD] += dv
            rows = pl.ds(pl.multiple_of(c * HD, HD), HD)
            dq_at[rows, :] = dq_at[rows, :] + dq if in_dq else dq
            return carry

        if n == 1 or nb == 1:
            for c in range(n):
                step(c, 0)
        else:
            lax.fori_loop(0, n, step, 0)
        if final and n > 1:
            for b in range(nb):
                out_refs[b][:, 0:HD] = out_refs[b][:, 0:HD] * SCALE
        if odd:
            for c, ref in enumerate(ins):
                dq_refs[0][c * HD : (c + 1) * HD, :] = ref[...]
            dq_refs[0][len(ins) * HD :, :] = dq_at[...].astype(dq_type)
        else:
            for c in range(n):
                dq_refs[c][...] = dq_at[c * HD : (c + 1) * HD, :].astype(dq_type[c])

    if odd:
        out_shape = [jax.ShapeDtypeStruct(((len(in_odd) + n) * HD, ROWS), dq_type)]
    else:
        out_shape = [jax.ShapeDtypeStruct((HD, ROWS), t) for t in dq_type]
    out_shape += [jax.ShapeDtypeStruct((BLOCK, 2 * HD), acc_type)] * nb
    outs = pl.pallas_call(
        body,
        out_shape=out_shape,
        scratch_shapes=message_scratch(n) + [pltpu.VMEM((n * HD, ROWS), jnp.float32)],
        input_output_aliases=aliases,
        compiler_params=pltpu.CompilerParams(vmem_limit_bytes=VMEM),
        cost_estimate=pl.CostEstimate(
            flops=n * 20 * ROWS * nb * BLOCK * HD,
            bytes_accessed=2 << 20,
            transcendentals=n * ROWS * nb * BLOCK,
        ),
        name=name,
    )(*operands)
    return list(outs[:n_dq]), list(outs[n_dq:])


def pair_kernel(got_ref, *refs):
    even_refs, keep_ref, send_refs = refs[: len(EVEN)], refs[len(EVEN)], refs[len(EVEN) + 1 :]
    away = 1 - 2 * (lax.axis_index("zp"))
    for i, offset in enumerate(EVEN):
        there = (offset - away + NZ) % NZ
        slot = jnp.int32(0)
        for j, odd in enumerate(ODD):
            slot = jnp.where(there == odd % NZ, j, slot)
        got = got_ref[pl.ds(pl.multiple_of(slot * HD, HD), HD), :].astype(jnp.float32)
        total = even_refs[i][...] + got
        if i == 0:
            keep_ref[...] = total
        else:
            send_refs[i - 1][...] = total.astype(jnp.bfloat16)


def pair(even, got):
    vm = pl.BlockSpec(memory_space=pltpu.VMEM)
    return pl.pallas_call(
        pair_kernel,
        out_shape=[jax.ShapeDtypeStruct((HD, ROWS), jnp.float32)]
        + [jax.ShapeDtypeStruct((HD, ROWS), jnp.bfloat16)] * 3,
        in_specs=[vm] * 5,
        out_specs=[vm] * 4,
        compiler_params=pltpu.CompilerParams(vmem_limit_bytes=SMALL),
        cost_estimate=pl.CostEstimate(flops=0, bytes_accessed=2 << 20, transcendentals=0),
        name="pair",
    )(got, *even)


def dispatch_kernel(owner_ref, own_ref, a_ref, b_ref, c_ref, out_ref, sum_ref, count_ref):
    f32 = jnp.float32
    total = own_ref[...] + a_ref[...].astype(f32) + b_ref[...].astype(f32) + c_ref[...].astype(f32)
    sum_ref[...] = total.astype(jnp.bfloat16)
    out_ref[...] = jnp.zeros_like(out_ref)
    for j in range(N_VID):
        count_ref[j] = 0

    first = vid_index() * FPD

    def place(f, carry):
        owner = owner_ref[first + f]
        slot = count_ref[owner]
        count_ref[owner] = slot + 1
        to = pl.multiple_of((owner * MOST + slot) * TPF, TPF)
        fr = pl.multiple_of(f * TPF, TPF)
        out_ref[pl.ds(to, TPF), :] = sum_ref[pl.ds(fr, TPF), :]
        return carry

    lax.fori_loop(0, FPD, place, 0)


def dispatch(owners, own, others):
    vm = pl.BlockSpec(memory_space=pltpu.VMEM)
    return pl.pallas_call(
        dispatch_kernel,
        out_shape=jax.ShapeDtypeStruct((SLOT_ROWS, 2 * HD), jnp.bfloat16),
        in_specs=[pl.BlockSpec(memory_space=pltpu.SMEM)] + [vm] * 4,
        out_specs=vm,
        scratch_shapes=[pltpu.VMEM((BLOCK, 2 * HD), jnp.bfloat16), pltpu.SMEM((N_VID,), jnp.int32)],
        compiler_params=pltpu.CompilerParams(vmem_limit_bytes=SMALL),
        cost_estimate=pl.CostEstimate(flops=0, bytes_accessed=2 << 20, transcendentals=0),
        name="dispatch",
    )(owners, own, *others)


PIECES = [(dx, other) for dx in (0, -1, 1, 2) for other in (False, True)]


def merge_kernel(_, wk_ref, wv_ref, out_ref):
    x, core = lax.axis_index("x"), lax.axis_index("core")
    for p, (dx, other) in enumerate(PIECES):
        by = 1 - core if other else core
        h = ((x + dx * (1 - 2 * by) + NX) % NX) * 2 + by
        at = pl.ds(pl.multiple_of(h * HD, HD), HD)
        out_ref[:, 2 * p * HD : (2 * p + 1) * HD] = wk_ref[:, at]
        out_ref[:, (2 * p + 1) * HD : (2 * p + 2) * HD] = wv_ref[:, at]


def merge(after, key_weight, value_weight):
    vm = pl.BlockSpec(memory_space=pltpu.VMEM)
    return pl.pallas_call(
        merge_kernel,
        out_shape=jax.ShapeDtypeStruct((key_weight.shape[0], 2 * KVH * HD), jnp.bfloat16),
        in_specs=[pl.BlockSpec(memory_space=pl.ANY), vm, vm],
        out_specs=vm,
        compiler_params=pltpu.CompilerParams(vmem_limit_bytes=SMALL),
        cost_estimate=pl.CostEstimate(flops=0, bytes_accessed=8 << 20, transcendentals=0),
        name="merge",
    )(after, key_weight, value_weight)


def project(name, pieces, first, weight, total=None):
    cols = weight.shape[0]
    n = len(pieces)
    final = total is not None
    tile = 256 if final else 512
    n_tile = SLOT_ROWS // tile
    feats = slice(2 * HD * first, 2 * HD * (first + n))

    def product(refs, w_ref, rows):
        a = jnp.concatenate([ref[rows, :] for ref in refs[:n]], axis=1)
        return dot32(a, w_ref[:, feats], NT)

    def body_first(*refs):
        w_ref, out_ref = refs[n:]
        for t in range(n_tile):
            rows = slice(t * tile, (t + 1) * tile)
            out_ref[rows, :] = product(refs, w_ref, rows)

    def body_final(*refs):
        w_ref, total_ref, out_ref, out_at, sems = refs[n:]
        copies = []
        for t in range(n_tile):
            rows = slice(t * tile, (t + 1) * tile)
            out_at[rows, :] = (total_ref[rows, :] + product(refs, w_ref, rows)).astype(jnp.bfloat16)
            copy = pltpu.make_async_copy(out_at.at[rows, :], out_ref.at[rows, :], sems.at[t])
            copy.start()
            copies.append(copy)
        for copy in copies:
            copy.wait()

    vm = pl.BlockSpec(memory_space=pltpu.VMEM)
    scratch = [pltpu.VMEM((SLOT_ROWS, cols), jnp.bfloat16), pltpu.SemaphoreType.DMA((n_tile,))]
    return pl.pallas_call(
        body_final if final else body_first,
        out_shape=jax.ShapeDtypeStruct((SLOT_ROWS, cols), jnp.bfloat16 if final else jnp.float32),
        in_specs=[vm] * (n + 1 + final),
        out_specs=pl.BlockSpec(memory_space=pltpu.HBM) if final else vm,
        scratch_shapes=scratch if final else [],
        compiler_params=pltpu.CompilerParams(vmem_limit_bytes=MIDDLE),
        cost_estimate=pl.CostEstimate(
            flops=4 * SLOT_ROWS * cols * n * HD, bytes_accessed=6 << 20, transcendentals=0
        ),
        name=name,
    )(*pieces, weight, *([total] if final else []))


def finish_kernel(keep_ref, a_ref, b_ref, c_ref, out_ref):
    total = keep_ref[...]
    for ref in (a_ref, b_ref, c_ref):
        total = total + ref[...].astype(jnp.float32)
    total = (total * SCALE).T
    for h in range(GROUP):
        out_ref[:, h * HD : (h + 1) * HD] = total[h * QLEN : (h + 1) * QLEN, :].astype(jnp.bfloat16)


def finish(keep, others):
    return pl.pallas_call(
        finish_kernel,
        out_shape=jax.ShapeDtypeStruct((QLEN, GROUP * HD), jnp.bfloat16),
        compiler_params=pltpu.CompilerParams(vmem_limit_bytes=SMALL),
        cost_estimate=pl.CostEstimate(flops=0, bytes_accessed=1 << 19, transcendentals=0),
        name="finish",
    )(keep, *others)


def on_device(
    queries,
    out_grad,
    log_totals,
    out_dots,
    lengths,
    vis_keys,
    vis_values,
    key_weight,
    value_weight,
    frame_owner,
):
    msg, kv0 = pack(
        lengths, queries, out_grad, log_totals, out_dots, vis_keys, vis_values
    )

    kv_up, kv_down = shift(kv0, "y", 1), shift(kv0, "y", -1)
    up1, down1 = shift(msg, "z", 1), shift(msg, "z", -1)
    away = [kv_up, kv_down, shift(kv0, "y", 2)]
    up2, down2 = shift(up1, "z", 1), shift(down1, "z", -1)
    bf16, f32 = jnp.bfloat16, jnp.float32
    none = [None] * NY

    near = [msg, up1, down1]
    dq, (own,) = attend("home_first", near, [kv0], none[:1], none[:3], [f32] * 3, f32, False)
    dq, acc = attend("away_near", near, away[:2], none[:2], dq, [f32] * 3, f32, False)
    up2, down2, acc[0] = lax.optimization_barrier((up2, down2, acc[0]))
    up3, down3 = shift(up2, "z", 1), shift(down2, "z", -1)
    two = [up2, down2]
    (dq_u2, dq_d2), acc = attend(
        "away_two", two, away, acc + [None], none[:2], [f32] * 2, f32, False
    )
    up3, down3, acc[0] = lax.optimization_barrier((up3, down3, acc[0]))
    far = shift(up3, "z", 1)
    (dq_0, dq_u1, dq_d1), acc[2:] = attend(
        "away_across", near, away[2:], acc[2:], dq, [f32, bf16, bf16], f32, False
    )
    three = [up3, down3]
    (odd,), acc = attend(
        "all_three", three, away + [kv0], acc + [own], none[:2], bf16, f32, False, (dq_u1, dq_d1)
    )
    own = acc.pop()
    (dq_4,), parts = attend("away_far", [far], away, acc, none[:1], [f32], bf16, True)

    part_up, part_down, part_far = parts
    back = (shift(part_far, "y", 2), shift(part_up, "y", -1), shift(part_down, "y", 1))
    got = lax.ppermute(odd, "zp", [(0, 1), (1, 0)])
    dq, (own,) = attend(
        "home_last", two + [far], [kv0], [own], [dq_u2, dq_d2, dq_4], [f32] * 3, f32, True
    )
    even = [dq_0, dq[1], dq[0], dq[2]]

    keep, *sends = pair(even, got)
    own, keep = lax.optimization_barrier((own, keep))

    outgoing = dispatch(frame_owner.reshape(-1), own, back)
    mine = lax.all_to_all(outgoing, Z + ("y",), split_axis=0, concat_axis=0, tiled=True)
    mine, *sends = lax.optimization_barrier((mine, *sends))

    first, second = shift_by_core(mine, 1), shift_by_core(mine, -1)
    others = [shift(rows, "z", offset) for rows, offset in zip(sends, EVEN[1:])]
    pieces = [mine, shift(mine, "core", 1)]
    first, second, others[0], others[1] = lax.optimization_barrier(
        (first, second, others[0], others[1])
    )
    across = shift_by_core(first, 1)
    for rows in (first, second):
        pieces += [rows, shift(rows, "core", 1)]
    weight = merge(first, key_weight, value_weight)
    total = project("project_near", pieces, 0, weight)
    others[2], total = lax.optimization_barrier((others[2], total))
    across, total = lax.optimization_barrier((across, total))
    pieces = [across, shift(across, "core", 1)]
    query_grad = finish(keep, others)
    total, query_grad = lax.optimization_barrier((total, query_grad))
    return query_grad, project("project_across", pieces, 6, weight, total)


def solution(mesh):
    devices = mesh.devices.reshape(NZ // 2, 2, NY, NX, 2)
    split = jax.sharding.Mesh(devices, Z + ("y", "x", "core"))
    vid, head = Z + ("y",), ("x", "core")
    in_specs = (
        P(vid, head),
        P(vid, head),
        P(head, vid),
        P(head, vid),
        P(),
        P(vid, head),
        P(vid, head),
        P(head, None),
        P(head, None),
        P(),
    )
    out_specs = (P(vid, head), P(vid, head))
    return jax.shard_map(
        on_device, mesh=split, in_specs=in_specs, out_specs=out_specs, check_vma=False
    )
```
